256 devices in a mesh: member: 8 (over y, z_hi), space: 32 (over x, z_lo, core).
Axes of the slice: x: 4, y: 4, z: 8 (z_hi: 2, z_lo: 4; z = z_hi * 4 + z_lo), core: 2. Of those that a mesh axis runs over, the one named last changes fastest.
Arguments:
- latent: bfloat16 [8, 32768, 1024], P('member', 'space'), may hold values from -6 to 6
- neighbours: int32 [4, 32768], P(None, 'space'), may hold values from 0 to 32767, as said below
- norm_gain: float32 [1024], replicated, may hold values from 0.1 to 1.9
- w_mix: bfloat16 [1024, 1024], replicated, may hold values from -0.1875 to 0.1875
- w_out: bfloat16 [1024, 100], replicated, may hold values from -0.1875 to 0.1875
- observed: float32 [100, 32768], P(None, 'space'), may hold values from -6 to 6
- cell_area: float32 [32768], P('space'), may hold values from 0.3 to 3
- var_weight: float32 [100], replicated, may hold values from 1 to 16
Outputs:
- crps_field: float32 [32768], P('space')
- grad_latent: bfloat16 [8, 32768, 1024], P('member', 'space')
- grad_mix: float32 [1024, 1024], P('space')
- grad_out: float32 [1024, 100], P('space')
The draws below stay inside these ranges and needn't reach their ends.
Inputs may be any that keep to these rules, and one draw needn't show every extreme that they name: neighbours[k, c] lies within 128 cells of c; neighbours[0, c] lies exactly 128 cells from c.
All inputs are finite; a program needn't handle non-finite values.
Results may differ from the reference program's by a relative error of at most 0.02.
Values may be sent and summed in bfloat16 or wider, within the bound.
No kernel may reach another device: no remote copies, remote signals or barrier semaphores. Data moves between devices by JAX's collectives and lax.ppermute only.
A program may use at most 128 MiB of HBM per device.

```python
import math
import jax
import jax.numpy as jnp
from jax import lax

D = 1024
VARS = 100
NBRS = 4
HALO = 128
CELLS = 32768
MEMBERS = 8


def draw_neighbours(key, part):
    key = jax.random.fold_in(key, 7)
    sign_key, offset_key = jax.random.split(key)
    cell_ids = jnp.arange(CELLS, dtype=jnp.int32)[None, :]
    sign_values = jax.random.randint(sign_key, (1, CELLS), 0, 2).astype(jnp.int32) * 2 - 1
    others = jax.random.randint(offset_key, (NBRS - 1, CELLS), -HALO, HALO + 1).astype(jnp.int32)
    offsets = jnp.concatenate([sign_values * HALO, others], axis=0)
    target = cell_ids + offsets
    inside = (target >= 0) & (target < CELLS)
    return jnp.where(inside, target, cell_ids - offsets).astype(jnp.int32)


def shard_levels(own_key, extent, pieces, smallest, top_value):
    gain, own = 1.0, jax.random.fold_in(own_key, 6)
    for axis_at, blocks in pieces:
        draws = jnp.exp(jax.random.uniform(jax.random.fold_in(own, axis_at), (blocks,), jnp.float32, smallest / len(pieces), top_value / len(pieces)))
        gain = gain * jnp.repeat(draws, extent[axis_at] // blocks).reshape([-1 if axis == axis_at else 1 for axis in range(len(extent))])
    return gain


def scatter_about(stream_key, extent, scale, reach, cuts=(), kind=jnp.bfloat16):
    drawn = jax.random.normal(stream_key, extent, jnp.float32) * scale
    if len(cuts) > 0:
        drawn = shard_levels(stream_key, extent, cuts, -0.22, 0.18) * drawn
    return jnp.clip(drawn, min=-reach, max=reach).astype(kind)


def setup_inputs(seed: int = 0) -> dict:
    streams_of = jax.random.split(jax.random.key(seed), 9)
    return {
        "latent": scatter_about(streams_of[0], (MEMBERS, CELLS, D), 1.0, 6.0, ((0, 8), (1, 32))),
        "neighbours": draw_neighbours(jax.random.fold_in(streams_of[8], 71), 0),
        "norm_gain": jnp.clip(1.0 + 0.18 * jax.random.normal(streams_of[2], (D,), jnp.float32), 0.1, 1.9),
        "w_mix": scatter_about(streams_of[3], (D, D), D ** -0.5, 0.1875),
        "w_out": scatter_about(streams_of[4], (D, VARS), D ** -0.5, 0.1875),
        "observed": scatter_about(streams_of[5], (VARS, CELLS), 1.0, 6.0, ((1, 32),), jnp.float32),
        "cell_area": jnp.clip(jnp.exp(math.log(3.0) - 2.3025851 * jax.random.uniform(streams_of[6], (CELLS,), jnp.float32) ** shard_levels(streams_of[6], (CELLS,), ((0, 32),), -0.2, 0.2)), 0.3, 3.0),
        "var_weight": jnp.clip(jnp.exp(jax.random.uniform(streams_of[7], (VARS,), jnp.float32, math.log(1.0), math.log(16.0))), 1.0, 16.0),
    }


smoothing = 0.1
root_two_pi = math.sqrt(2.0 / math.pi)
cubic = 0.044715
epsilon = 1e-06
fair_shift = 0.05

def gelu_parts(preact):
    tanh_input = root_two_pi * (preact + cubic * preact * preact * preact)
    tanh_value = jnp.tanh(tanh_input)
    activation = 0.5 * preact * (1.0 + tanh_value)
    derivative = 0.5 * (1.0 + tanh_value) + 0.5 * preact * (1.0 - tanh_value * tanh_value) * root_two_pi * (1.0 + 3.0 * cubic * preact * preact)
    return (activation, derivative)

def decoder_forward(center, aggregate, norm_gain, w_mix):
    combined = center.astype(jnp.float32) + aggregate
    inverse = lax.rsqrt(lax.optimization_barrier(jnp.mean(combined * combined, axis=1, keepdims=True)) + epsilon)
    normed = (combined * inverse * norm_gain).astype(jnp.bfloat16)
    preact = jnp.dot(normed, w_mix, preferred_element_type=jnp.float32)
    activation, derivative = gelu_parts(preact)
    hidden = (combined + activation).astype(jnp.bfloat16)
    return (combined, inverse, normed, derivative, hidden)

def decoder_backward(g_member, combined, inverse, derivative, norm_gain, w_mix, w_out):
    d_hidden = lax.dot_general(g_member, w_out, (((0,), (1,)), ((), ())), preferred_element_type=jnp.float32)
    d_pre = (d_hidden * derivative).astype(jnp.bfloat16)
    d_normed = lax.dot_general(d_pre, w_mix, (((1,), (1,)), ((), ())), preferred_element_type=jnp.float32)
    scaled = d_normed * norm_gain
    d_combined = d_hidden + inverse * scaled - combined * (inverse * inverse * inverse) * lax.optimization_barrier(jnp.mean(combined * scaled, axis=1, keepdims=True))
    return (d_pre, d_combined)

def reference(latent, neighbours, norm_gain, w_mix, w_out, observed, cell_area, var_weight):
    member_count = latent.shape[0]
    cell_count = latent.shape[1]
    flat_edges = neighbours.reshape(-1)

    def aggregate_of(center):
        gathered = jnp.take(center, flat_edges, axis=0).astype(jnp.float32)
        return lax.optimization_barrier(jnp.sum(gathered.reshape(NBRS, cell_count, D), axis=0)) / NBRS

    def predict(center):
        parts = decoder_forward(center, aggregate_of(center), norm_gain, w_mix)
        return lax.dot_general(w_out, parts[4], (((0,), (1,)), ((), ())), preferred_element_type=jnp.float32)
    preds = lax.map(predict, latent)
    cell_weight = var_weight[:, None] * cell_area[None, :]
    fair_weight = 1.0 - fair_shift / member_count
    pair_coef = fair_weight / (2.0 * member_count * (member_count - 1))
    obs_gap = preds - observed[None]
    smooth_obs = jnp.sqrt(obs_gap * obs_gap + smoothing * smoothing)
    member_ids = jnp.arange(member_count, dtype=jnp.int32)

    def pair_sums(member_pos):
        pair_gap = preds[member_pos][None] - preds
        smooth = jnp.sqrt(pair_gap * pair_gap + smoothing * smoothing)
        distinct = (member_ids != member_pos)[:, None, None]
        return (lax.optimization_barrier(jnp.sum(jnp.where(distinct, smooth, 0.0), axis=0)), lax.optimization_barrier(jnp.sum(jnp.where(distinct, pair_gap / smooth, 0.0), axis=0)))
    pair_s, pair_ds = lax.map(pair_sums, member_ids)
    member_term = smooth_obs / member_count - pair_coef * pair_s
    crps_field = lax.optimization_barrier(jnp.sum(cell_weight[None] * member_term, axis=(0, 1)))
    g_pred = (cell_weight[None] * (obs_gap / smooth_obs / member_count - 2.0 * pair_coef * pair_ds)).astype(jnp.bfloat16)

    def backward_member(totals, inputs):
        center, g_member = inputs
        combined, inverse, normed, derivative, hidden = decoder_forward(center, aggregate_of(center), norm_gain, w_mix)
        d_pre, d_combined = decoder_backward(g_member, combined, inverse, derivative, norm_gain, w_mix, w_out)
        spread = jnp.zeros((cell_count, D), jnp.float32).at[flat_edges].add(jnp.tile(d_combined / NBRS, (NBRS, 1)))
        grad_center = (d_combined + spread).astype(jnp.bfloat16)
        part_mix = lax.dot_general(normed, d_pre, (((0,), (0,)), ((), ())), preferred_element_type=jnp.float32)
        part_out = lax.dot_general(hidden, g_member, (((0,), (1,)), ((), ())), preferred_element_type=jnp.float32)
        return ((totals[0] + part_mix, totals[1] + part_out), grad_center)
    start_totals = (jnp.zeros((D, D), jnp.float32), jnp.zeros((D, VARS), jnp.float32))
    totals, grad_latent = lax.scan(backward_member, start_totals, (latent, g_pred))
    grad_scale = 1.0 / math.sqrt(member_count * cell_count)
    return (crps_field, grad_latent, totals[0] * grad_scale, totals[1] * grad_scale)
```

```python
import math

import jax
import jax.numpy as jnp
from jax import lax
from jax.experimental import pallas as pl
from jax.experimental.pallas import tpu as pltpu
from jax.sharding import PartitionSpec as P

D = 1024
VARS = 100
NBRS = 4
HALO = 128
ROWS = 112
MEMBERS = 8
CELLS = 1024
BLK = 256
STEPS = CELLS // BLK
PIECE = CELLS // MEMBERS
WIDE = D + 128

smoothing = 0.1
root_two_pi = math.sqrt(2.0 / math.pi)
cubic = 0.044715
epsilon = 1e-06
fair_shift = 0.05
fair_weight = 1.0 - fair_shift / MEMBERS
pair_coef = fair_weight / (2.0 * MEMBERS * (MEMBERS - 1))

bf16 = jnp.bfloat16
f32 = jnp.float32
VMEM_LIMIT = 56 * 1024 * 1024


def whole(shape):
    return pl.BlockSpec(shape, lambda *_: (0,) * len(shape), pipeline_mode=pl.Buffered(1))


def edge_matrix(nb_ref, base, scale):
    local = (nb_ref[...] - base).T
    column = lax.broadcasted_iota(jnp.int32, (BLK, BLK + 2 * HALO), 1)
    count = jnp.zeros((BLK, BLK + 2 * HALO), f32)
    for k in range(NBRS):
        count = count + jnp.where(column == local[:, k : k + 1], scale, 0.0)
    return count


def forward_kernel(
    nb_ref, lat_ref, low_ref, high_ref, gain_ref, mix_ref, out_ref,
    normed_ref, hidden_ref, deriv_ref, inv_ref, pred_ref, send_ref, ext,
):
    step = pl.program_id(0)

    @pl.when(step == 0)
    def _():
        ext[0:HALO] = low_ref[...]
        ext[HALO : HALO + CELLS] = lat_ref[...]
        ext[HALO + CELLS :] = high_ref[...]

    first = pl.multiple_of(step * BLK, BLK)
    base = lax.axis_index("space") * CELLS - HALO + first
    edges = edge_matrix(nb_ref, base, 1.0).astype(bf16)
    window = ext[pl.ds(first, BLK + 2 * HALO)]
    total = jnp.dot(edges, window, preferred_element_type=f32)
    combined = window[HALO : HALO + BLK].astype(f32) + total * (1.0 / NBRS)
    inverse = lax.rsqrt(jnp.mean(combined * combined, axis=1, keepdims=True) + epsilon)
    normed = (combined * inverse * gain_ref[...]).astype(bf16)
    normed_ref[...] = normed
    inv_ref[...] = inverse
    x = jnp.dot(normed, mix_ref[...], preferred_element_type=f32)
    square = x * x
    tanh = jnp.tanh(x * (root_two_pi + (root_two_pi * cubic) * square))
    half = 0.5 + 0.5 * tanh
    activation = x * half
    deriv_ref[...] = (
        half + activation * (1.0 - tanh) * (root_two_pi + (3.0 * root_two_pi * cubic) * square)
    ).astype(bf16)
    hidden = (combined + activation).astype(bf16)
    hidden_ref[...] = hidden
    pred = lax.dot_general(
        out_ref[...], hidden, (((1,), (1,)), ((), ())), preferred_element_type=f32
    )
    pred_ref[...] = pred
    rounded = pred.astype(bf16)
    for j in range(BLK // PIECE):
        send_ref[j] = rounded[:, j * PIECE : (j + 1) * PIECE]


def forward(neighbours, center, low, high, gain, w_mix, w_out):
    rows = pl.BlockSpec((BLK, D), lambda i: (i, 0))
    return pl.pallas_call(
        forward_kernel,
        grid=(STEPS,),
        in_specs=[
            pl.BlockSpec((NBRS, BLK), lambda i: (0, i)),
            whole((CELLS, D)),
            whole((HALO, D)),
            whole((HALO, D)),
            whole((1, D)),
            whole((D, D)),
            whole((ROWS, D)),
        ],
        out_specs=[
            rows,
            rows,
            rows,
            pl.BlockSpec((BLK, 1), lambda i: (i, 0)),
            pl.BlockSpec((ROWS, BLK), lambda i: (0, i)),
            pl.BlockSpec((BLK // PIECE, ROWS, PIECE), lambda i: (i, 0, 0)),
        ],
        out_shape=[
            jax.ShapeDtypeStruct((CELLS, D), bf16),
            jax.ShapeDtypeStruct((CELLS, D), bf16),
            jax.ShapeDtypeStruct((CELLS, D), bf16),
            jax.ShapeDtypeStruct((CELLS, 1), f32),
            jax.ShapeDtypeStruct((ROWS, CELLS), f32),
            jax.ShapeDtypeStruct((MEMBERS, ROWS, PIECE), bf16),
        ],
        scratch_shapes=[pltpu.VMEM((CELLS + 2 * HALO, D), bf16)],
        compiler_params=pltpu.CompilerParams(vmem_limit_bytes=VMEM_LIMIT),
        cost_estimate=pl.CostEstimate(
            flops=4 * CELLS * D * D, bytes_accessed=14 << 20, transcendentals=CELLS * D
        ),
        name="forward",
    )(neighbours, center, low, high, gain, w_mix, w_out)


def pair_kernel(pred_ref, obs_ref, area_ref, weight_ref, back_ref):
    first = pl.multiple_of(lax.axis_index("member") * PIECE, PIECE)
    area = area_ref[:, pl.ds(first, PIECE)]
    loss = jnp.zeros((16, PIECE), f32)
    for tile in range(ROWS // 16):
        rows = slice(16 * tile, 16 * tile + 16)
        preds = [pred_ref[m, rows].astype(f32) for m in range(MEMBERS)]
        observed = obs_ref[rows, pl.ds(first, PIECE)]
        slopes = [jnp.zeros((16, PIECE), f32)] * MEMBERS
        near = jnp.zeros((16, PIECE), f32)
        apart = jnp.zeros((16, PIECE), f32)
        for m in range(MEMBERS):
            gap = preds[m] - observed
            value = gap * gap + smoothing * smoothing
            near = near + value * lax.rsqrt(value)
            for k in range(m + 1, MEMBERS):
                gap = preds[m] - preds[k]
                value = gap * gap + smoothing * smoothing
                root = lax.rsqrt(value)
                apart = apart + value * root
                slope = gap * root
                slopes[m] = slopes[m] + slope
                slopes[k] = slopes[k] - slope
        loss = loss + weight_ref[rows] * (
            near * (1.0 / MEMBERS) - (2.0 * pair_coef) * apart
        )
        if tile < ROWS // 16 - 1:
            for m in range(MEMBERS):
                back_ref[m, rows] = slopes[m].astype(bf16)
    loss = jnp.sum(loss, axis=0, keepdims=True) * area
    high = loss.astype(bf16).astype(f32)
    middle = (loss - high).astype(bf16).astype(f32)
    low = loss - high - middle
    row = lax.broadcasted_iota(jnp.int32, (16, PIECE), 0) - (VARS - (ROWS - 16))
    for m in range(MEMBERS):
        tail = jnp.where(row < 0, slopes[m], 0.0)
        for at, part in enumerate((high, middle, low)):
            tail = jnp.where(row == at, part, tail)
        back_ref[m, ROWS - 16 : ROWS] = tail.astype(bf16)


def pair_terms(preds, observed, area, weight):
    return pl.pallas_call(
        pair_kernel,
        out_shape=jax.ShapeDtypeStruct((MEMBERS, ROWS, PIECE), bf16),
        cost_estimate=pl.CostEstimate(
            flops=1 << 24, bytes_accessed=1 << 20, transcendentals=1 << 20
        ),
        compiler_params=pltpu.CompilerParams(vmem_limit_bytes=VMEM_LIMIT),
        name="pairs",
    )(preds, observed, area, weight)


def weights_kernel(
    pos_ref, pair_ref, pred_ref, obs_ref, area_ref, weight_ref, out_ref, deriv_ref, hidden_ref, normed_ref,
    g_ref, pre_ref, loss_ref, keep_ref, send_ref, pre_all, out_sum,
):
    step = pl.program_id(0)

    @pl.when(step < STEPS)
    def _():
        pair = jnp.concatenate([pair_ref[j] for j in range(BLK // PIECE)], axis=1).astype(f32)
        loss_ref[...] = jnp.sum(pair[VARS : VARS + 3], axis=0, keepdims=True)
        gap = pred_ref[...] - obs_ref[...]
        slope = gap * lax.rsqrt(gap * gap + smoothing * smoothing)
        g = (
            weight_ref[...]
            * area_ref[...]
            * (slope * (1.0 / MEMBERS) - (2.0 * pair_coef) * pair)
        ).astype(bf16)
        g_ref[...] = g
        d_hidden = lax.dot_general(
            g, out_ref[...], (((0,), (0,)), ((), ())), preferred_element_type=f32
        )
        d_pre = (d_hidden * deriv_ref[...].astype(f32)).astype(bf16)
        pre_ref[...] = d_pre
        pre_all[pl.ds(pl.multiple_of(step * BLK, BLK), BLK)] = d_pre
        part = jnp.dot(g, hidden_ref[...], preferred_element_type=f32)

        @pl.when(step == 0)
        def _():
            out_sum[0:ROWS] = part
            out_sum[ROWS:] = jnp.zeros((128 - ROWS, D), f32)

        @pl.when(step > 0)
        def _():
            out_sum[0:ROWS] += part

    @pl.when(step >= STEPS)
    def _():
        x_at = lax.rem(pos_ref[0] + step - STEPS, 4)
        mix = lax.dot_general(
            normed_ref[...], pre_all[...], (((0,), (0,)), ((), ())), preferred_element_type=f32
        ).astype(bf16)
        out = out_sum[:, pl.ds(pl.multiple_of(x_at * BLK, BLK), BLK)].T.astype(bf16)
        mine = pos_ref[2] == 0
        for z in range(4):
            at = lax.rem(z + 4 - pos_ref[1], 4)
            for source, lanes in ((mix, slice(0, D)), (out, slice(D, WIDE))):
                even = source[64 * z : 64 * z + 32]
                odd = source[64 * z + 32 : 64 * z + 64]
                keep_ref[0, at, :, lanes] = jnp.where(mine, even, odd)
                send_ref[0, at, :, lanes] = jnp.where(mine, odd, even)


def weight_parts(pos, pair, pred, observed, area, weight, w_out, deriv, hidden, normed):
    first = lambda i: jnp.minimum(i, STEPS - 1)
    later = lambda i: jnp.maximum(i - STEPS, 0)
    rows = pl.BlockSpec((BLK, D), lambda i, pos: (first(i), 0))
    columns = pl.BlockSpec((ROWS, BLK), lambda i, pos: (0, first(i)))
    line = pl.BlockSpec((1, BLK), lambda i, pos: (0, first(i)))
    share = pl.BlockSpec((1, 4, 32, WIDE), lambda i, pos: (later(i), 0, 0, 0))
    return pl.pallas_call(
        weights_kernel,
        grid_spec=pltpu.PrefetchScalarGridSpec(
            num_scalar_prefetch=1,
            grid=(2 * STEPS,),
            in_specs=[
                pl.BlockSpec((BLK // PIECE, ROWS, PIECE), lambda i, pos: (first(i), 0, 0)),
                columns,
                columns,
                line,
                whole((ROWS, 1)),
                whole((ROWS, D)),
                rows,
                rows,
                pl.BlockSpec((CELLS, BLK), lambda i, pos: (0, lax.rem(pos[0] + later(i), 4))),
            ],
            out_specs=[columns, rows, line, share, share],
            scratch_shapes=[pltpu.VMEM((CELLS, D), bf16), pltpu.VMEM((128, D), f32)],
        ),
        out_shape=[
            jax.ShapeDtypeStruct((ROWS, CELLS), bf16),
            jax.ShapeDtypeStruct((CELLS, D), bf16),
            jax.ShapeDtypeStruct((1, CELLS), f32),
            jax.ShapeDtypeStruct((4, 4, 32, WIDE), bf16),
            jax.ShapeDtypeStruct((4, 4, 32, WIDE), bf16),
        ],
        compiler_params=pltpu.CompilerParams(vmem_limit_bytes=VMEM_LIMIT),
        cost_estimate=pl.CostEstimate(
            flops=3 * CELLS * D * D, bytes_accessed=14 << 20, transcendentals=0
        ),
        name="weights",
    )(pos, pair, pred, observed, area, weight, w_out, deriv, hidden, normed)


def latent_kernel(
    nb_ref, g_ref, out_ref, pre_ref, mix_ref, gain_ref, normed_ref, inv_ref,
    grad_ref, low_ref, high_ref, carry,
):
    step = pl.program_id(0)
    d_hidden = lax.dot_general(
        g_ref[...], out_ref[...], (((0,), (0,)), ((), ())), preferred_element_type=f32
    )
    d_normed = lax.dot_general(
        pre_ref[...], mix_ref[...], (((1,), (1,)), ((), ())), preferred_element_type=f32
    )
    gain = gain_ref[...]
    normed = normed_ref[...].astype(f32)
    mean = jnp.mean(normed * d_normed, axis=1, keepdims=True)
    d_combined = d_hidden + inv_ref[...] * (d_normed * gain - normed * (1.0 / gain) * mean)
    first = pl.multiple_of(step * BLK, BLK)
    base = lax.axis_index("space") * CELLS - HALO + first
    edges = edge_matrix(nb_ref, base, 1.0 / NBRS)
    row = lax.broadcasted_iota(jnp.int32, edges.shape, 0)
    column = lax.broadcasted_iota(jnp.int32, edges.shape, 1)
    edges = (edges + jnp.where(column == row + HALO, 1.0, 0.0)).astype(bf16)
    spread = lax.dot_general(
        edges, d_combined.astype(bf16), (((0,), (0,)), ((), ())), preferred_element_type=f32
    )

    @pl.when(step == 0)
    def _():
        low_ref[...] = spread[0:HALO].astype(bf16)
        grad_ref[0:HALO] = spread[HALO:BLK].astype(bf16)

    @pl.when(step > 0)
    def _():
        grad_ref[pl.ds(pl.multiple_of(first - HALO, HALO), BLK)] = (
            spread[0:BLK] + carry[...]
        ).astype(bf16)

    carry[...] = spread[BLK:]

    @pl.when(step == STEPS - 1)
    def _():
        grad_ref[CELLS - HALO :] = spread[BLK : BLK + HALO].astype(bf16)
        high_ref[...] = spread[BLK + HALO :].astype(bf16)


def latent_parts(neighbours, g, w_out, d_pre, w_mix, gain, normed, inverse):
    rows = pl.BlockSpec((BLK, D), lambda i: (i, 0))
    rim = jax.ShapeDtypeStruct((HALO, D), bf16)
    return pl.pallas_call(
        latent_kernel,
        grid=(STEPS,),
        in_specs=[
            pl.BlockSpec((NBRS, BLK), lambda i: (0, i)),
            pl.BlockSpec((ROWS, BLK), lambda i: (0, i)),
            whole((ROWS, D)),
            rows,
            whole((D, D)),
            whole((1, D)),
            rows,
            pl.BlockSpec((BLK, 1), lambda i: (i, 0)),
        ],
        out_specs=[whole((CELLS, D)), whole((HALO, D)), whole((HALO, D))],
        out_shape=[jax.ShapeDtypeStruct((CELLS, D), bf16), rim, rim],
        scratch_shapes=[pltpu.VMEM((BLK, D), f32)],
        compiler_params=pltpu.CompilerParams(vmem_limit_bytes=VMEM_LIMIT),
        cost_estimate=pl.CostEstimate(
            flops=4 * CELLS * D * D, bytes_accessed=10 << 20, transcendentals=0
        ),
        name="latent",
    )(neighbours, g, w_out, d_pre, w_mix, gain, normed, inverse)


def rim_kernel(grad_ref, low_ref, high_ref, out_ref):
    step = pl.program_id(0)
    other = jnp.where(step == 0, low_ref[...], high_ref[...])
    out_ref[...] = (grad_ref[...].astype(f32) + other.astype(f32)).astype(bf16)


def add_rims(grad, low, high):
    rim = pl.BlockSpec((HALO, D), lambda i: (i * (CELLS // HALO - 1), 0))
    return pl.pallas_call(
        rim_kernel,
        grid=(2,),
        in_specs=[rim, whole((HALO, D)), whole((HALO, D))],
        out_specs=rim,
        out_shape=jax.ShapeDtypeStruct((CELLS, D), bf16),
        input_output_aliases={0: 0},
        cost_estimate=pl.CostEstimate(flops=1 << 18, bytes_accessed=3 << 19, transcendentals=0),
        name="rims",
    )(grad, low, high)


def along(value, axis, move):
    pairs = [(i, move(i)) for i in range(lax.axis_size(axis))]
    return lax.ppermute(value, axis, [pair for pair in pairs if pair[1] is not None])


def next_band(i):
    return i + 1 if i < 31 else None


def last_band(i):
    return i - 1 if i > 0 else None


def summed(parts):
    total = parts[0].astype(f32)
    for part in parts[1:]:
        total = total + part.astype(f32)
    return total


def shards(latent, neighbours, norm_gain, w_mix, w_out, observed, cell_area, var_weight):
    space = lax.axis_index("space")
    pos = jnp.stack([space // 8, space // 2 % 4, space % 2]).astype(jnp.int32)
    center = latent[0]
    low = along(center[CELLS - HALO :], "space", next_band)
    high = along(center[:HALO], "space", last_band)
    gain = norm_gain.reshape(1, D)
    area = cell_area.reshape(1, CELLS)
    out_t = jnp.pad(w_out.T, ((0, ROWS - VARS), (0, 0)))
    observed = jnp.pad(observed, ((0, ROWS - VARS), (0, 0)))
    weight = jnp.pad(var_weight, (0, ROWS - VARS)).reshape(ROWS, 1)

    normed, hidden, deriv, inverse, pred, pieces = forward(
        neighbours, center, low, high, gain, w_mix, out_t
    )
    pieces = lax.all_to_all(pieces, "member", 0, 0, tiled=True)
    pairs = pair_terms(pieces, observed, area, weight)
    pairs = lax.all_to_all(pairs, "member", 0, 0, tiled=True)
    g, d_pre, losses, keep, send = weight_parts(
        pos, pairs, pred, observed, area, weight, out_t, deriv, hidden, normed
    )
    got = along(send, "space", lambda i: i ^ 1)
    grad, low_rim, high_rim = latent_parts(
        neighbours, g, out_t, d_pre, w_mix, gain, normed, inverse
    )
    from_above = along(low_rim, "space", last_band)
    from_below = along(high_rim, "space", next_band)
    grad = add_rims(grad, from_below, from_above)

    def over_x(k):
        return along(summed([keep[k], got[k]]).astype(bf16), "space", lambda i: (i + 8 * k) % 32)

    share = summed([keep[0], got[0]] + [over_x(k) for k in (1, 2, 3)]).astype(bf16)

    def over_z(k):
        return along(share[k], "space", lambda i: i // 8 * 8 + (i + 2 * k) % 8)

    share = summed([share[0]] + [over_z(k) for k in (1, 2, 3)]).astype(bf16)
    share = summed(
        [share] + [along(share, "member", lambda i: (i + 2 * k) % 8) for k in (1, 2, 3)]
    ).astype(bf16)
    totals = summed([share, along(share, "member", lambda i: i ^ 1)])
    grad_scale = 1.0 / math.sqrt(MEMBERS * CELLS * 32)
    return (
        losses.reshape(CELLS),
        grad[None],
        totals[:, :D] * grad_scale,
        totals[:, D : D + VARS] * grad_scale,
    )


def solution(mesh):
    return jax.shard_map(
        shards,
        mesh=mesh,
        in_specs=(
            P("member", "space", None),
            P(None, "space"),
            P(),
            P(),
            P(),
            P(None, "space"),
            P("space"),
            P(),
        ),
        out_specs=(P("space"), P("member", "space", None), P("space", None), P("space", None)),
        check_vma=False,
    )
```

```python
import math

import jax
import jax.numpy as jnp
from jax import lax
from jax.experimental import pallas as pl
from jax.experimental.pallas import tpu as pltpu
from jax.sharding import PartitionSpec as P

D = 1024
VARS = 100
NBRS = 4
HALO = 128
ROWS = 112
MEMBERS = 8
CELLS = 1024
BLK = 256
STEPS = CELLS // BLK
PIECE = CELLS // MEMBERS
WIDE = D + 128

smoothing = 0.1
root_two_pi = math.sqrt(2.0 / math.pi)
cubic = 0.044715
epsilon = 1e-06
fair_shift = 0.05
fair_weight = 1.0 - fair_shift / MEMBERS
pair_coef = fair_weight / (2.0 * MEMBERS * (MEMBERS - 1))

bf16 = jnp.bfloat16
f32 = jnp.float32
VMEM_LIMIT = 56 * 1024 * 1024


def whole(shape):
    return pl.BlockSpec(shape, lambda *_: (0,) * len(shape), pipeline_mode=pl.Buffered(1))


def edge_matrix(neighbours, base, width, scale):
    local = (neighbours - base).T
    column = lax.broadcasted_iota(jnp.int32, (local.shape[0], width), 1)
    count = jnp.zeros(column.shape, f32)
    for k in range(NBRS):
        count = count + jnp.where(column == local[:, k : k + 1], scale, 0.0)
    return count


def gathered(neighbours, base, window):
    edges = edge_matrix(neighbours, base, window.shape[0], 1.0).astype(bf16)
    total = jnp.dot(edges, window, preferred_element_type=f32)
    own = window[HALO : HALO + edges.shape[0]].astype(f32)
    return own + total * (1.0 / NBRS)


def decode(combined, gain, mix, out_t, normed_ref, hidden_ref, deriv_ref, inv_ref, pred_ref, send_ref):
    inverse = lax.rsqrt(jnp.mean(combined * combined, axis=1, keepdims=True) + epsilon)
    normed = (combined * inverse * gain).astype(bf16)
    normed_ref[...] = normed
    inv_ref[...] = inverse
    x = jnp.dot(normed, mix, preferred_element_type=f32)
    square = x * x
    tanh = jnp.tanh(x * (root_two_pi + (root_two_pi * cubic) * square))
    half = 0.5 + 0.5 * tanh
    activation = x * half
    deriv_ref[...] = (
        half + activation * (1.0 - tanh) * (root_two_pi + (3.0 * root_two_pi * cubic) * square)
    ).astype(bf16)
    hidden = (combined + activation).astype(bf16)
    hidden_ref[...] = hidden
    pred = lax.dot_general(out_t, hidden, (((1,), (1,)), ((), ())), preferred_element_type=f32)
    pred_ref[...] = pred
    rounded = pred.astype(bf16)
    for j in range(BLK // PIECE):
        send_ref[j] = rounded[:, j * PIECE : (j + 1) * PIECE]


def interior_kernel(
    nb0_ref, nb1_ref, lat_ref, gain_ref, mix_ref, out_ref,
    out_t_ref, normed_ref, hidden_ref, deriv_ref, inv_ref, pred_ref, send_ref,
):
    step = pl.program_id(0)

    @pl.when(step == 0)
    def _():
        row = lax.broadcasted_iota(jnp.int32, (ROWS, VARS), 0)
        column = lax.broadcasted_iota(jnp.int32, (ROWS, VARS), 1)
        pick = jnp.where(row == column, 1.0, 0.0).astype(bf16)
        out_t_ref[...] = lax.dot_general(
            pick, out_ref[...], (((1,), (1,)), ((), ())), preferred_element_type=f32
        ).astype(bf16)

    first = pl.multiple_of(step * BLK, BLK)
    neighbours = jnp.concatenate([nb0_ref[...], nb1_ref[...]], axis=1)
    base = lax.axis_index("space") * CELLS + first
    combined = gathered(neighbours, base, lat_ref[pl.ds(first, BLK + 2 * HALO)])
    decode(
        combined, gain_ref[...], mix_ref[...], out_t_ref[...],
        normed_ref, hidden_ref, deriv_ref, inv_ref, pred_ref, send_ref,
    )


def rim_cells_kernel(
    nb0_ref, nb1_ref, last_ref, head_ref, low_ref, high_ref, gain_ref, mix_ref, out_t_ref,
    *refs,
):
    start = lax.axis_index("space") * CELLS
    window = jnp.concatenate([last_ref[...], high_ref[...]], axis=0)
    last = gathered(nb0_ref[...], start + CELLS - BLK, window)
    window = jnp.concatenate([low_ref[...], head_ref[...]], axis=0)
    head = gathered(nb1_ref[...], start - HALO, window)
    combined = jnp.concatenate([last, head], axis=0)
    decode(combined, gain_ref[...], mix_ref[...], out_t_ref[...], *refs[6:])


def forward(neighbours, center, low, high, gain, w_mix, w_out):
    shapes = [
        jax.ShapeDtypeStruct((CELLS, D), bf16),
        jax.ShapeDtypeStruct((CELLS, D), bf16),
        jax.ShapeDtypeStruct((CELLS, D), bf16),
        jax.ShapeDtypeStruct((CELLS, 1), f32),
        jax.ShapeDtypeStruct((ROWS, CELLS), f32),
        jax.ShapeDtypeStruct((MEMBERS, ROWS, PIECE), bf16),
    ]

    def blocks(at):
        rows = pl.BlockSpec((BLK, D), lambda i: (at(i), 0))
        return [
            rows,
            rows,
            rows,
            pl.BlockSpec((BLK, 1), lambda i: (at(i), 0)),
            pl.BlockSpec((ROWS, BLK), lambda i: (0, at(i))),
            pl.BlockSpec((BLK // PIECE, ROWS, PIECE), lambda i: (at(i), 0, 0)),
        ]

    def edges_at(column):
        return pl.BlockSpec((NBRS, PIECE), lambda i: (0, column(i)))

    def cost(steps):
        return pl.CostEstimate(
            flops=steps * 4 * BLK * D * D, bytes_accessed=steps * 3 << 20, transcendentals=steps * BLK * D
        )

    out_t, *arrays = pl.pallas_call(
        interior_kernel,
        grid=(STEPS - 1,),
        in_specs=[
            edges_at(lambda i: 2 * i + 1),
            edges_at(lambda i: 2 * i + 2),
            whole((CELLS, D)),
            whole((1, D)),
            whole((D, D)),
            whole((D, VARS)),
        ],
        out_specs=[whole((ROWS, D))] + blocks(lambda i: i),
        out_shape=[jax.ShapeDtypeStruct((ROWS, D), bf16)] + shapes,
        compiler_params=pltpu.CompilerParams(vmem_limit_bytes=VMEM_LIMIT),
        cost_estimate=cost(STEPS - 1),
        name="interior",
    )(neighbours, neighbours, center, gain, w_mix, w_out)
    arrays = pl.pallas_call(
        rim_cells_kernel,
        grid=(1,),
        in_specs=[
            edges_at(lambda i: MEMBERS - 1),
            edges_at(lambda i: 0),
            pl.BlockSpec((BLK, D), lambda i: (STEPS - 1, 0)),
            pl.BlockSpec((BLK, D), lambda i: (0, 0)),
            whole((HALO, D)),
            whole((HALO, D)),
            whole((1, D)),
            whole((D, D)),
            whole((ROWS, D)),
        ]
        + [pl.BlockSpec(memory_space=pl.ANY)] * len(shapes),
        out_specs=blocks(lambda i: STEPS - 1),
        out_shape=shapes,
        input_output_aliases={9 + i: i for i in range(len(shapes))},
        compiler_params=pltpu.CompilerParams(vmem_limit_bytes=VMEM_LIMIT),
        cost_estimate=cost(1),
        name="rim_cells",
    )(neighbours, neighbours, center, center, low, high, gain, w_mix, out_t, *arrays)
    return out_t, arrays


def pair_kernel(pred_ref, obs_ref, area_ref, weight_ref, back_ref):
    piece = lax.rem(lax.axis_index("member") + 1, MEMBERS)
    first = pl.multiple_of(piece * PIECE, PIECE)
    area = area_ref[:, pl.ds(first, PIECE)]
    loss = jnp.zeros((16, PIECE), f32)
    for tile in range(ROWS // 16):
        rows = slice(16 * tile, 16 * tile + 16)
        preds = [pred_ref[m, rows].astype(f32) for m in range(MEMBERS)]
        observed = obs_ref[rows, pl.ds(first, PIECE)]
        slopes = [jnp.zeros((16, PIECE), f32)] * MEMBERS
        near = jnp.zeros((16, PIECE), f32)
        apart = jnp.zeros((16, PIECE), f32)
        for m in range(MEMBERS):
            gap = preds[m] - observed
            value = gap * gap + smoothing * smoothing
            near = near + value * lax.rsqrt(value)
            for k in range(m + 1, MEMBERS):
                gap = preds[m] - preds[k]
                value = gap * gap + smoothing * smoothing
                root = lax.rsqrt(value)
                apart = apart + value * root
                slope = gap * root
                slopes[m] = slopes[m] + slope
                slopes[k] = slopes[k] - slope
        loss = loss + weight_ref[rows] * (
            near * (1.0 / MEMBERS) - (2.0 * pair_coef) * apart
        )
        if tile < ROWS // 16 - 1:
            for m in range(MEMBERS):
                back_ref[m, rows] = slopes[m].astype(bf16)
    loss = jnp.sum(loss, axis=0, keepdims=True) * area
    high = loss.astype(bf16).astype(f32)
    middle = (loss - high).astype(bf16).astype(f32)
    low = loss - high - middle
    row = lax.broadcasted_iota(jnp.int32, (16, PIECE), 0) - (VARS - (ROWS - 16))
    for m in range(MEMBERS):
        tail = jnp.where(row < 0, slopes[m], 0.0)
        for at, part in enumerate((high, middle, low)):
            tail = jnp.where(row == at, part, tail)
        back_ref[m, ROWS - 16 : ROWS] = tail.astype(bf16)


def pair_terms(preds, observed, area, weight):
    return pl.pallas_call(
        pair_kernel,
        out_shape=jax.ShapeDtypeStruct((MEMBERS, ROWS, PIECE), bf16),
        cost_estimate=pl.CostEstimate(
            flops=1 << 24, bytes_accessed=1 << 20, transcendentals=1 << 20
        ),
        compiler_params=pltpu.CompilerParams(vmem_limit_bytes=VMEM_LIMIT),
        name="pairs",
    )(preds, observed, area, weight)


def weights_kernel(
    pos_ref, pair_ref, pred_ref, obs0_ref, obs1_ref, area0_ref, area1_ref, weight_ref, out_ref, deriv_ref, hidden_ref, normed_ref,
    g_ref, pre_ref, loss_ref, keep_ref, send_ref, pre_all, out_sum,
):
    step = pl.program_id(0)

    @pl.when(step < STEPS)
    def _():
        pair = jnp.concatenate([pair_ref[j] for j in range(BLK // PIECE)], axis=1).astype(f32)
        loss = jnp.sum(pair[VARS : VARS + 3], axis=0, keepdims=True)
        for j in range(BLK // PIECE):
            at = lax.rem(2 * step + 1 + j, MEMBERS) * PIECE
            loss_ref[:, pl.ds(pl.multiple_of(at, PIECE), PIECE)] = loss[:, j * PIECE : (j + 1) * PIECE]
        area = jnp.concatenate([area0_ref[...], area1_ref[...]], axis=1)
        gap = pred_ref[...] - jnp.concatenate([obs0_ref[...], obs1_ref[...]], axis=1)
        slope = gap * lax.rsqrt(gap * gap + smoothing * smoothing)
        g = (
            weight_ref[...]
            * area
            * (slope * (1.0 / MEMBERS) - (2.0 * pair_coef) * pair)
        ).astype(bf16)
        g_ref[...] = g
        d_hidden = lax.dot_general(
            g, out_ref[...], (((0,), (0,)), ((), ())), preferred_element_type=f32
        )
        d_pre = (d_hidden * deriv_ref[...].astype(f32)).astype(bf16)
        pre_ref[...] = d_pre
        pre_all[pl.ds(pl.multiple_of(step * BLK, BLK), BLK)] = d_pre
        part = jnp.dot(g, hidden_ref[...], preferred_element_type=f32)

        @pl.when(step == 0)
        def _():
            out_sum[0:ROWS] = part
            out_sum[ROWS:] = jnp.zeros((128 - ROWS, D), f32)

        @pl.when(step > 0)
        def _():
            out_sum[0:ROWS] += part

    @pl.when(step >= STEPS)
    def _():
        x_at = lax.rem(pos_ref[0] + step - STEPS, 4)
        mix = lax.dot_general(
            normed_ref[...], pre_all[...], (((0,), (0,)), ((), ())), preferred_element_type=f32
        ).astype(bf16)
        out = out_sum[:, pl.ds(pl.multiple_of(x_at * BLK, BLK), BLK)].T.astype(bf16)
        mine = pos_ref[2] == 0
        for z in range(4):
            at = lax.rem(z + 4 - pos_ref[1], 4)
            for source, lanes in ((mix, slice(0, D)), (out, slice(D, WIDE))):
                even = source[64 * z : 64 * z + 32]
                odd = source[64 * z + 32 : 64 * z + 64]
                keep_ref[0, at, :, lanes] = jnp.where(mine, even, odd)
                send_ref[0, at, :, lanes] = jnp.where(mine, odd, even)


def weight_parts(pos, pair, pred, observed, area, weight, w_out, deriv, hidden, normed):
    first = lambda i: jnp.minimum(i, STEPS - 1)
    later = lambda i: jnp.maximum(i - STEPS, 0)
    rows = pl.BlockSpec((BLK, D), lambda i, pos: (first(i), 0))
    columns = pl.BlockSpec((ROWS, BLK), lambda i, pos: (0, first(i)))
    left = lambda i, pos: (0, 2 * first(i) + 1)
    right = lambda i, pos: (0, lax.rem(2 * first(i) + 2, MEMBERS))
    share = pl.BlockSpec((1, 4, 32, WIDE), lambda i, pos: (later(i), 0, 0, 0))
    return pl.pallas_call(
        weights_kernel,
        grid_spec=pltpu.PrefetchScalarGridSpec(
            num_scalar_prefetch=1,
            grid=(2 * STEPS,),
            in_specs=[
                pl.BlockSpec((BLK // PIECE, ROWS, PIECE), lambda i, pos: (first(i), 0, 0)),
                columns,
                pl.BlockSpec((ROWS, PIECE), left),
                pl.BlockSpec((ROWS, PIECE), right),
                pl.BlockSpec((1, PIECE), left),
                pl.BlockSpec((1, PIECE), right),
                whole((ROWS, 1)),
                whole((ROWS, D)),
                rows,
                rows,
                pl.BlockSpec((CELLS, BLK), lambda i, pos: (0, lax.rem(pos[0] + later(i), 4))),
            ],
            out_specs=[columns, rows, whole((1, CELLS)), share, share],
            scratch_shapes=[pltpu.VMEM((CELLS, D), bf16), pltpu.VMEM((128, D), f32)],
        ),
        out_shape=[
            jax.ShapeDtypeStruct((ROWS, CELLS), bf16),
            jax.ShapeDtypeStruct((CELLS, D), bf16),
            jax.ShapeDtypeStruct((1, CELLS), f32),
            jax.ShapeDtypeStruct((4, 4, 32, WIDE), bf16),
            jax.ShapeDtypeStruct((4, 4, 32, WIDE), bf16),
        ],
        compiler_params=pltpu.CompilerParams(vmem_limit_bytes=VMEM_LIMIT),
        cost_estimate=pl.CostEstimate(
            flops=3 * CELLS * D * D, bytes_accessed=14 << 20, transcendentals=0
        ),
        name="weights",
    )(pos, pair, pred, observed, observed, area, area, weight, w_out, deriv, hidden, normed)


def latent_kernel(
    nb0_ref, nb1_ref, g_ref, out_ref, pre_ref, mix_ref, gain_ref, normed_ref, inv_ref,
    grad_ref, low_ref, high_ref, carry, tail,
):
    step = pl.program_id(0)
    d_hidden = lax.dot_general(
        g_ref[...], out_ref[...], (((0,), (0,)), ((), ())), preferred_element_type=f32
    )
    d_normed = lax.dot_general(
        pre_ref[...], mix_ref[...], (((1,), (1,)), ((), ())), preferred_element_type=f32
    )
    gain = gain_ref[...]
    normed = normed_ref[...].astype(f32)
    mean = jnp.mean(normed * d_normed, axis=1, keepdims=True)
    d_combined = d_hidden + inv_ref[...] * (d_normed * gain - normed * (1.0 / gain) * mean)
    d_combined = d_combined.astype(bf16)
    start = lax.axis_index("space") * CELLS

    def spread(neighbours, base, cells, width):
        edges = edge_matrix(neighbours, base, width, 1.0 / NBRS)
        row = lax.broadcasted_iota(jnp.int32, edges.shape, 0)
        column = lax.broadcasted_iota(jnp.int32, edges.shape, 1)
        edges = (edges + jnp.where(column == row + HALO, 1.0, 0.0)).astype(bf16)
        return lax.dot_general(
            edges, cells, (((0,), (0,)), ((), ())), preferred_element_type=f32
        )

    @pl.when(step == 0)
    def _():
        last = spread(nb0_ref[...], start + CELLS - BLK, d_combined[0:HALO], BLK + HALO)
        tail[...] = last[0:BLK]
        high_ref[...] = last[BLK:].astype(bf16)
        head = spread(nb1_ref[...], start - HALO, d_combined[HALO:], BLK + HALO)
        low_ref[...] = head[0:HALO].astype(bf16)
        carry[...] = head[HALO:]

    @pl.when(step > 0)
    def _():
        first = pl.multiple_of((step - 1) * BLK, BLK)
        neighbours = jnp.concatenate([nb0_ref[...], nb1_ref[...]], axis=1)
        part = spread(neighbours, start + first, d_combined, BLK + 2 * HALO)
        grad_ref[pl.ds(first, BLK)] = (part[0:BLK] + carry[...]).astype(bf16)
        carry[...] = part[BLK:]

    @pl.when(step == STEPS - 1)
    def _():
        grad_ref[CELLS - BLK :] = (carry[...] + tail[...]).astype(bf16)


def latent_parts(neighbours, g, w_out, d_pre, w_mix, gain, normed, inverse):
    at = lambda i: lax.rem(i + STEPS - 1, STEPS)
    rows = pl.BlockSpec((BLK, D), lambda i: (at(i), 0))
    rim = jax.ShapeDtypeStruct((HALO, D), bf16)
    return pl.pallas_call(
        latent_kernel,
        grid=(STEPS,),
        in_specs=[
            pl.BlockSpec((NBRS, PIECE), lambda i: (0, 2 * at(i) + 1)),
            pl.BlockSpec((NBRS, PIECE), lambda i: (0, lax.rem(2 * at(i) + 2, MEMBERS))),
            pl.BlockSpec((ROWS, BLK), lambda i: (0, at(i))),
            whole((ROWS, D)),
            rows,
            whole((D, D)),
            whole((1, D)),
            rows,
            pl.BlockSpec((BLK, 1), lambda i: (at(i), 0)),
        ],
        out_specs=[whole((CELLS, D)), whole((HALO, D)), whole((HALO, D))],
        out_shape=[jax.ShapeDtypeStruct((CELLS, D), bf16), rim, rim],
        scratch_shapes=[pltpu.VMEM((BLK, D), f32), pltpu.VMEM((BLK, D), f32)],
        compiler_params=pltpu.CompilerParams(vmem_limit_bytes=VMEM_LIMIT),
        cost_estimate=pl.CostEstimate(
            flops=4 * CELLS * D * D, bytes_accessed=10 << 20, transcendentals=0
        ),
        name="latent",
    )(neighbours, neighbours, g, w_out, d_pre, w_mix, gain, normed, inverse)


def rim_kernel(grad_ref, low_ref, high_ref, out_ref):
    step = pl.program_id(0)
    other = jnp.where(step == 0, low_ref[...], high_ref[...])
    out_ref[...] = (grad_ref[...].astype(f32) + other.astype(f32)).astype(bf16)


def add_rims(grad, low, high):
    rim = pl.BlockSpec((HALO, D), lambda i: (i * (CELLS // HALO - 1), 0))
    return pl.pallas_call(
        rim_kernel,
        grid=(2,),
        in_specs=[rim, whole((HALO, D)), whole((HALO, D))],
        out_specs=rim,
        out_shape=jax.ShapeDtypeStruct((CELLS, D), bf16),
        input_output_aliases={0: 0},
        cost_estimate=pl.CostEstimate(flops=1 << 18, bytes_accessed=3 << 19, transcendentals=0),
        name="rims",
    )(grad, low, high)


def along(value, axis, move):
    pairs = [(i, move(i)) for i in range(lax.axis_size(axis))]
    return lax.ppermute(value, axis, [pair for pair in pairs if pair[1] is not None])


def next_band(i):
    return i + 1 if i < 31 else None


def last_band(i):
    return i - 1 if i > 0 else None


def summed(parts):
    total = parts[0].astype(f32)
    for part in parts[1:]:
        total = total + part.astype(f32)
    return total


def shards(latent, neighbours, norm_gain, w_mix, w_out, observed, cell_area, var_weight):
    space = lax.axis_index("space")
    pos = jnp.stack([space // 8, space // 2 % 4, space % 2]).astype(jnp.int32)
    center = latent[0]
    low = along(center[CELLS - HALO :], "space", next_band)
    high = along(center[:HALO], "space", last_band)
    gain = norm_gain.reshape(1, D)
    area = cell_area.reshape(1, CELLS)
    observed = jnp.pad(observed, ((0, ROWS - VARS), (0, 0)))
    weight = jnp.pad(var_weight, (0, ROWS - VARS)).reshape(ROWS, 1)

    out_t, arrays = forward(neighbours, center, low, high, gain, w_mix, w_out)
    normed, hidden, deriv, inverse, pred, pieces = arrays
    pieces = lax.all_to_all(pieces, "member", 0, 0, tiled=True)
    pairs = pair_terms(pieces, observed, area, weight)
    pairs = lax.all_to_all(pairs, "member", 0, 0, tiled=True)
    g, d_pre, losses, keep, send = weight_parts(
        pos, pairs, pred, observed, area, weight, out_t, deriv, hidden, normed
    )
    got = along(send, "space", lambda i: i ^ 1)

    def over_x(k):
        return along(summed([keep[k], got[k]]).astype(bf16), "space", lambda i: (i + 8 * k) % 32)

    arrived = [over_x(k) for k in (1, 2, 3)]
    grad, low_rim, high_rim = latent_parts(
        neighbours, g, out_t, d_pre, w_mix, gain, normed, inverse
    )
    arrived, grad = lax.optimization_barrier((arrived, grad))
    from_above = along(low_rim, "space", last_band)
    from_below = along(high_rim, "space", next_band)
    share = summed([keep[0], got[0]] + arrived).astype(bf16)

    def over_z(k):
        return along(share[k], "space", lambda i: i // 8 * 8 + (i + 2 * k) % 8)

    arrived = [over_z(k) for k in (1, 2, 3)]
    arrived, from_above, from_below = lax.optimization_barrier((arrived, from_above, from_below))
    share = summed([share[0]] + arrived).astype(bf16)
    arrived = [along(share, "member", lambda i: (i + 2 * k) % 8) for k in (1, 2, 3)]
    grad = add_rims(grad, from_below, from_above)
    arrived, grad = lax.optimization_barrier((arrived, grad))
    share = summed([share] + arrived).astype(bf16)
    totals = summed([share, along(share, "member", lambda i: i ^ 1)])
    grad_scale = 1.0 / math.sqrt(MEMBERS * CELLS * 32)
    return (
        losses.reshape(CELLS),
        grad[None],
        totals[:, :D] * grad_scale,
        totals[:, D : D + VARS] * grad_scale,
    )


def solution(mesh):
    return jax.shard_map(
        shards,
        mesh=mesh,
        in_specs=(
            P("member", "space", None),
            P(None, "space"),
            P(),
            P(),
            P(),
            P(None, "space"),
            P("space"),
            P(),
        ),
        out_specs=(P("space"), P("member", "space", None), P("space", None), P("space", None)),
        check_vma=False,
    )
```

```python
import math

import jax
import jax.numpy as jnp
from jax import lax
from jax.experimental import pallas as pl
from jax.experimental.pallas import tpu as pltpu
from jax.sharding import PartitionSpec as P

D = 1024
VARS = 100
NBRS = 4
HALO = 128
ROWS = 112
MEMBERS = 8
CELLS = 1024
BLK = 256
STEPS = CELLS // BLK
PIECE = CELLS // MEMBERS
WIDE = D + 128

smoothing = 0.1
root_two_pi = math.sqrt(2.0 / math.pi)
cubic = 0.044715
epsilon = 1e-06
fair_shift = 0.05
fair_weight = 1.0 - fair_shift / MEMBERS
pair_coef = fair_weight / (2.0 * MEMBERS * (MEMBERS - 1))

bf16 = jnp.bfloat16
f32 = jnp.float32
VMEM_LIMIT = 24 * 1024 * 1024


def whole(shape):
    return pl.BlockSpec(shape, lambda *_: (0,) * len(shape), pipeline_mode=pl.Buffered(1))


def edge_matrix(neighbours, base, width):
    local = (neighbours - base).T
    shape = (local.shape[0], width)
    column = lax.broadcasted_iota(jnp.int32, shape, 1)
    row = lax.broadcasted_iota(jnp.int32, shape, 0)
    count = jnp.where(column == row + HALO, float(NBRS), 0.0)
    for k in range(NBRS):
        count = count + jnp.where(column == local[:, k : k + 1], 1.0, 0.0)
    return count.astype(bf16)


def gathered(edges, window):
    return jnp.dot(edges, window, preferred_element_type=f32) * (1.0 / NBRS)


def decode(combined, gain, mix, out_t, normed_ref, hidden_ref, deriv_ref, inv_ref, pred_ref, send_ref):
    inverse = lax.rsqrt(jnp.mean(combined * combined, axis=1, keepdims=True) + epsilon)
    normed = (combined * inverse * gain).astype(bf16)
    normed_ref[...] = normed
    inv_ref[...] = inverse
    x = jnp.dot(normed, mix, preferred_element_type=f32)
    square = x * x
    tanh = jnp.tanh(x * (root_two_pi + (root_two_pi * cubic) * square))
    half = 0.5 + 0.5 * tanh
    activation = x * half
    deriv_ref[...] = (
        half + activation * (1.0 - tanh) * (root_two_pi + (3.0 * root_two_pi * cubic) * square)
    ).astype(bf16)
    hidden = (combined + activation).astype(bf16)
    hidden_ref[...] = hidden
    pred = lax.dot_general(out_t, hidden, (((1,), (1,)), ((), ())), preferred_element_type=f32)
    pred_ref[...] = pred
    rounded = pred.astype(bf16)
    for j in range(BLK // PIECE):
        send_ref[j] = rounded[:, j * PIECE : (j + 1) * PIECE]


def interior_kernel(
    nb0_ref, nb1_ref, gain_ref, out_ref, lat_hbm, mix_hbm,
    out_t_ref, ends_ref, mix_out, edges_ref, normed_ref, hidden_ref, deriv_ref, inv_ref, pred_ref,
    *refs,
):
    send_ref, lat, mix, sems = refs
    step = pl.program_id(0)
    copies = [
        pltpu.make_async_copy(
            lat_hbm.at[i * BLK : (i + 1) * BLK], lat.at[i * BLK : (i + 1) * BLK], sems.at[i]
        )
        for i in range(STEPS)
    ] + [
        pltpu.make_async_copy(
            mix_hbm.at[i * BLK : (i + 1) * BLK], mix.at[i * BLK : (i + 1) * BLK], sems.at[STEPS + i]
        )
        for i in range(STEPS)
    ]
    first = pl.multiple_of(step * BLK, BLK)

    @pl.when(step == 0)
    def _():
        for at in (0, 1, 4, 5, 6, 7, 2, 3):
            copies[at].start()
        row = lax.broadcasted_iota(jnp.int32, (ROWS, VARS), 0)
        column = lax.broadcasted_iota(jnp.int32, (ROWS, VARS), 1)
        pick = jnp.where(row == column, 1.0, 0.0).astype(bf16)
        out_t_ref[...] = lax.dot_general(
            pick, out_ref[...], (((1,), (0,)), ((), ())), preferred_element_type=f32
        ).astype(bf16)

    neighbours = jnp.concatenate([nb0_ref[...], nb1_ref[...]], axis=1)
    base = lax.axis_index("space") * CELLS + first
    edges = edge_matrix(neighbours, base, BLK + 2 * HALO)
    edges_ref[...] = edges

    @pl.when(step == 0)
    def _():
        for copy in copies[0:2] + copies[STEPS:]:
            copy.wait()

    @pl.when(step == 1)
    def _():
        copies[2].wait()

    @pl.when(step == 2)
    def _():
        copies[3].wait()

    combined = gathered(edges, lat[pl.ds(first, BLK + 2 * HALO)])
    decode(
        combined, gain_ref[...], mix[...], out_t_ref[...],
        normed_ref, hidden_ref, deriv_ref, inv_ref, pred_ref, send_ref,
    )

    @pl.when(step == STEPS - 2)
    def _():
        ends_ref[0:BLK] = lat[0:BLK]
        ends_ref[BLK:] = lat[CELLS - BLK :]
        mix_out[...] = mix[...]


def rim_cells_kernel(
    nb0_ref, nb1_ref, ends_ref, near_ref, far_ref, gain_ref, mix_ref, out_t_ref,
    *refs,
):
    edges_ref, *refs = refs[len(refs) // 2 :]
    space = lax.axis_index("space")
    start = space * CELLS
    first_core = lax.rem(space, 2) == 0
    low = jnp.where(first_core, far_ref[...], near_ref[...])
    high = jnp.where(first_core, near_ref[...], far_ref[...])
    last_edges = edge_matrix(nb0_ref[...], start + CELLS - BLK, BLK + HALO)
    head_edges = edge_matrix(nb1_ref[...], start - HALO, BLK + HALO)
    edges_ref[0:HALO, 0 : BLK + HALO] = last_edges
    edges_ref[HALO:, 0 : BLK + HALO] = head_edges
    last = gathered(last_edges, jnp.concatenate([ends_ref[BLK:], high], axis=0))
    head = gathered(head_edges, jnp.concatenate([low, ends_ref[0:BLK]], axis=0))
    combined = jnp.concatenate([last, head], axis=0)
    decode(combined, gain_ref[...], mix_ref[...], out_t_ref[...], *refs)


def in_hbm(value):
    return pltpu.with_memory_space_constraint(value, pltpu.HBM)


def forward(neighbours, center, near, far, gain, w_mix, w_out):
    shapes = [
        pltpu.HBM((CELLS, BLK + 2 * HALO), bf16),
        pltpu.HBM((CELLS, D), bf16),
        pltpu.HBM((CELLS, D), bf16),
        pltpu.HBM((CELLS, D), bf16),
        pltpu.HBM((CELLS, 1), f32),
        pltpu.HBM((ROWS, CELLS), f32),
        pltpu.HBM((MEMBERS, ROWS, PIECE), bf16),
    ]

    def blocks(at):
        rows = pl.BlockSpec((BLK, D), lambda i: (at(i), 0))
        return [
            pl.BlockSpec((BLK, BLK + 2 * HALO), lambda i: (at(i), 0)),
            rows,
            rows,
            rows,
            pl.BlockSpec((BLK, 1), lambda i: (at(i), 0)),
            pl.BlockSpec((ROWS, BLK), lambda i: (0, at(i))),
            pl.BlockSpec((BLK // PIECE, ROWS, PIECE), lambda i: (at(i), 0, 0)),
        ]

    def edges_at(column):
        return pl.BlockSpec((NBRS, PIECE), lambda i: (0, column(i)))

    def cost(steps):
        return pl.CostEstimate(
            flops=steps * 4 * BLK * D * D, bytes_accessed=steps * 3 << 20, transcendentals=steps * BLK * D
        )

    neighbours, gain = in_hbm(neighbours), in_hbm(gain)
    out_t, ends, mix, *arrays = pl.pallas_call(
        interior_kernel,
        grid=(STEPS - 1,),
        in_specs=[
            edges_at(lambda i: 2 * i + 1),
            edges_at(lambda i: 2 * i + 2),
            whole((1, D)),
            whole((VARS, D)),
            pl.BlockSpec(memory_space=pltpu.HBM),
            pl.BlockSpec(memory_space=pltpu.HBM),
        ],
        out_specs=[whole((ROWS, D)), whole((2 * BLK, D)), whole((D, D))] + blocks(lambda i: i),
        out_shape=[
            jax.ShapeDtypeStruct((ROWS, D), bf16),
            jax.ShapeDtypeStruct((2 * BLK, D), bf16),
            jax.ShapeDtypeStruct((D, D), bf16),
        ]
        + shapes,
        scratch_shapes=[
            pltpu.VMEM((CELLS, D), bf16),
            pltpu.VMEM((D, D), bf16),
            pltpu.SemaphoreType.DMA((2 * STEPS,)),
        ],
        compiler_params=pltpu.CompilerParams(vmem_limit_bytes=VMEM_LIMIT),
        cost_estimate=cost(STEPS - 1),
        name="interior",
    )(neighbours, neighbours, gain, in_hbm(w_out), in_hbm(center), in_hbm(w_mix))
    arrays = pl.pallas_call(
        rim_cells_kernel,
        grid=(1,),
        in_specs=[
            edges_at(lambda i: MEMBERS - 1),
            edges_at(lambda i: 0),
            whole((2 * BLK, D)),
            whole((HALO, D)),
            whole((HALO, D)),
            whole((1, D)),
            whole((D, D)),
            whole((ROWS, D)),
        ]
        + [pl.BlockSpec(memory_space=pltpu.HBM)] * len(shapes),
        out_specs=blocks(lambda i: STEPS - 1),
        out_shape=shapes,
        input_output_aliases={8 + i: i for i in range(len(shapes))},
        compiler_params=pltpu.CompilerParams(vmem_limit_bytes=VMEM_LIMIT),
        cost_estimate=cost(1),
        name="rim_cells",
    )(neighbours, neighbours, ends, near, far, gain, mix, out_t, *arrays)
    return out_t, mix, arrays


def pair_kernel(pred_ref, obs_ref, area_ref, weight_ref, back_ref):
    piece = lax.rem(lax.axis_index("member") + 1, MEMBERS)
    first = pl.multiple_of(piece * PIECE, PIECE)
    area = area_ref[:, pl.ds(first, PIECE)]
    loss = jnp.zeros((16, PIECE), f32)
    for tile in range(ROWS // 16):
        rows = slice(16 * tile, 16 * tile + 16)
        preds = [pred_ref[m, rows].astype(f32) for m in range(MEMBERS)]
        observed = obs_ref[rows, pl.ds(first, PIECE)]
        slopes = [jnp.zeros((16, PIECE), f32)] * MEMBERS
        near = jnp.zeros((16, PIECE), f32)
        apart = jnp.zeros((16, PIECE), f32)
        for m in range(MEMBERS):
            gap = preds[m] - observed
            value = gap * gap + smoothing * smoothing
            near = near + value * lax.rsqrt(value)
            for k in range(m + 1, MEMBERS):
                gap = preds[m] - preds[k]
                value = gap * gap + smoothing * smoothing
                root = lax.rsqrt(value)
                apart = apart + value * root
                slope = gap * root
                slopes[m] = slopes[m] + slope
                slopes[k] = slopes[k] - slope
        loss = loss + weight_ref[rows] * (
            near * (1.0 / MEMBERS) - (2.0 * pair_coef) * apart
        )
        if tile < ROWS // 16 - 1:
            for m in range(MEMBERS):
                back_ref[m, rows] = slopes[m].astype(bf16)
    loss = jnp.sum(loss, axis=0, keepdims=True) * area
    high = loss.astype(bf16).astype(f32)
    middle = (loss - high).astype(bf16).astype(f32)
    low = loss - high - middle
    row = lax.broadcasted_iota(jnp.int32, (16, PIECE), 0) - (VARS - (ROWS - 16))
    for m in range(MEMBERS):
        tail = jnp.where(row < 0, slopes[m], 0.0)
        for at, part in enumerate((high, middle, low)):
            tail = jnp.where(row == at, part, tail)
        back_ref[m, ROWS - 16 : ROWS] = tail.astype(bf16)


def pair_terms(preds, observed, area, weight):
    return pl.pallas_call(
        pair_kernel,
        out_shape=pltpu.HBM((MEMBERS, ROWS, PIECE), bf16),
        cost_estimate=pl.CostEstimate(
            flops=1 << 24, bytes_accessed=1 << 20, transcendentals=1 << 20
        ),
        compiler_params=pltpu.CompilerParams(vmem_limit_bytes=VMEM_LIMIT),
        name="pairs",
    )(preds, in_hbm(observed), area, weight)


def weights_kernel(
    pos_ref, pair_ref, pred_ref, obs0_ref, obs1_ref, area0_ref, area1_ref, weight_ref, out_ref, deriv_ref, hidden_ref, normed_ref,
    g_ref, pre_ref, loss_ref, keep_ref, send_ref, pre_all, out_sum,
):
    step = pl.program_id(0)

    @pl.when(step < STEPS)
    def _():
        pair = jnp.concatenate([pair_ref[j] for j in range(BLK // PIECE)], axis=1).astype(f32)
        loss = jnp.sum(pair[VARS : VARS + 3], axis=0, keepdims=True)
        for j in range(BLK // PIECE):
            at = lax.rem(2 * step + 1 + j, MEMBERS) * PIECE
            loss_ref[:, pl.ds(pl.multiple_of(at, PIECE), PIECE)] = loss[:, j * PIECE : (j + 1) * PIECE]
        area = jnp.concatenate([area0_ref[...], area1_ref[...]], axis=1)
        gap = pred_ref[...] - jnp.concatenate([obs0_ref[...], obs1_ref[...]], axis=1)
        slope = gap * lax.rsqrt(gap * gap + smoothing * smoothing)
        g = (
            weight_ref[...]
            * area
            * (slope * (1.0 / MEMBERS) - (2.0 * pair_coef) * pair)
        ).astype(bf16)
        g_ref[...] = g
        d_hidden = lax.dot_general(
            g, out_ref[...], (((0,), (0,)), ((), ())), preferred_element_type=f32
        )
        d_pre = (d_hidden * deriv_ref[...].astype(f32)).astype(bf16)
        pre_ref[...] = d_pre
        pre_all[pl.ds(pl.multiple_of(step * BLK, BLK), BLK)] = d_pre
        part = jnp.dot(g, hidden_ref[...], preferred_element_type=f32)

        @pl.when(step == 0)
        def _():
            out_sum[0:ROWS] = part
            out_sum[ROWS:] = jnp.zeros((128 - ROWS, D), f32)

        @pl.when(step > 0)
        def _():
            out_sum[0:ROWS] += part

    @pl.when(step >= STEPS)
    def _():
        x_at = lax.rem(pos_ref[0] + step - STEPS, 4)
        mix = lax.dot_general(
            normed_ref[...], pre_all[...], (((0,), (0,)), ((), ())), preferred_element_type=f32
        ).astype(bf16)
        out = out_sum[:, pl.ds(pl.multiple_of(x_at * BLK, BLK), BLK)].T.astype(bf16)
        mine = pos_ref[2] == 0
        for z in range(4):
            at = lax.rem(z + 4 - pos_ref[1], 4)
            for source, lanes in ((mix, slice(0, D)), (out, slice(D, WIDE))):
                even = source[64 * z : 64 * z + 32]
                odd = source[64 * z + 32 : 64 * z + 64]
                keep_ref[0, at, :, lanes] = jnp.where(mine, even, odd)
                send_ref[0, at, :, lanes] = jnp.where(mine, odd, even)


def weight_parts(pos, pair, pred, observed, area, weight, w_out, deriv, hidden, normed):
    first = lambda i: jnp.minimum(i, STEPS - 1)
    later = lambda i: jnp.maximum(i - STEPS, 0)
    rows = pl.BlockSpec((BLK, D), lambda i, pos: (first(i), 0))
    columns = pl.BlockSpec((ROWS, BLK), lambda i, pos: (0, first(i)))
    left = lambda i, pos: (0, 2 * first(i) + 1)
    right = lambda i, pos: (0, lax.rem(2 * first(i) + 2, MEMBERS))
    share = pl.BlockSpec((1, 4, 32, WIDE), lambda i, pos: (later(i), 0, 0, 0))
    return pl.pallas_call(
        weights_kernel,
        grid_spec=pltpu.PrefetchScalarGridSpec(
            num_scalar_prefetch=1,
            grid=(2 * STEPS,),
            in_specs=[
                pl.BlockSpec((BLK // PIECE, ROWS, PIECE), lambda i, pos: (first(i), 0, 0)),
                columns,
                pl.BlockSpec((ROWS, PIECE), left),
                pl.BlockSpec((ROWS, PIECE), right),
                pl.BlockSpec((1, PIECE), left),
                pl.BlockSpec((1, PIECE), right),
                whole((ROWS, 1)),
                whole((ROWS, D)),
                rows,
                rows,
                pl.BlockSpec((CELLS, BLK), lambda i, pos: (0, lax.rem(pos[0] + later(i), 4))),
            ],
            out_specs=[columns, rows, whole((1, CELLS)), share, share],
            scratch_shapes=[pltpu.VMEM((CELLS, D), bf16), pltpu.VMEM((128, D), f32)],
        ),
        out_shape=[
            jax.ShapeDtypeStruct((ROWS, CELLS), bf16),
            jax.ShapeDtypeStruct((CELLS, D), bf16),
            jax.ShapeDtypeStruct((1, CELLS), f32),
            jax.ShapeDtypeStruct((4, 4, 32, WIDE), bf16),
            jax.ShapeDtypeStruct((4, 4, 32, WIDE), bf16),
        ],
        compiler_params=pltpu.CompilerParams(vmem_limit_bytes=VMEM_LIMIT),
        cost_estimate=pl.CostEstimate(
            flops=3 * CELLS * D * D, bytes_accessed=14 << 20, transcendentals=0
        ),
        name="weights",
    )(
        pos, pair, in_hbm(pred), in_hbm(observed), in_hbm(observed), area, area, weight, w_out,
        in_hbm(deriv), in_hbm(hidden), in_hbm(normed),
    )


def latent_kernel(
    edges_ref, g_ref, out_ref, pre_ref, mix_ref, gain_ref, normed_ref, inv_ref,
    grad_ref, near_ref, far_ref, carry, tail,
):
    step = pl.program_id(0)
    d_hidden = lax.dot_general(
        g_ref[...], out_ref[...], (((0,), (0,)), ((), ())), preferred_element_type=f32
    )
    d_normed = lax.dot_general(
        pre_ref[...], mix_ref[...], (((1,), (1,)), ((), ())), preferred_element_type=f32
    )
    gain = gain_ref[...]
    normed = normed_ref[...].astype(f32)
    mean = jnp.mean(normed * d_normed, axis=1, keepdims=True)
    d_combined = d_hidden + inv_ref[...] * (d_normed * gain - normed * (1.0 / gain) * mean)
    d_combined = d_combined.astype(bf16)

    def spread(edges, cells):
        return (1.0 / NBRS) * lax.dot_general(
            edges, cells, (((0,), (0,)), ((), ())), preferred_element_type=f32
        )

    @pl.when(step == 0)
    def _():
        last = spread(edges_ref[0:HALO, 0 : BLK + HALO], d_combined[0:HALO])
        tail[...] = last[0:BLK]
        head = spread(edges_ref[HALO:, 0 : BLK + HALO], d_combined[HALO:])
        carry[...] = head[HALO:]
        high, low = last[BLK:].astype(bf16), head[0:HALO].astype(bf16)
        first_core = lax.rem(lax.axis_index("space"), 2) == 0
        near_ref[...] = jnp.where(first_core, high, low)
        far_ref[...] = jnp.where(first_core, low, high)

    @pl.when(step > 0)
    def _():
        first = pl.multiple_of((step - 1) * BLK, BLK)
        part = spread(edges_ref[...], d_combined)
        grad_ref[pl.ds(first, BLK)] = (part[0:BLK] + carry[...]).astype(bf16)
        carry[...] = part[BLK:]

    @pl.when(step == STEPS - 1)
    def _():
        grad_ref[CELLS - BLK :] = (carry[...] + tail[...]).astype(bf16)


def latent_parts(edges, g, w_out, d_pre, w_mix, gain, normed, inverse):
    at = lambda i: lax.rem(i + STEPS - 1, STEPS)
    rows = pl.BlockSpec((BLK, D), lambda i: (at(i), 0))
    rim = jax.ShapeDtypeStruct((HALO, D), bf16)
    return pl.pallas_call(
        latent_kernel,
        grid=(STEPS,),
        in_specs=[
            pl.BlockSpec((BLK, BLK + 2 * HALO), lambda i: (at(i), 0)),
            pl.BlockSpec((ROWS, BLK), lambda i: (0, at(i))),
            whole((ROWS, D)),
            rows,
            whole((D, D)),
            whole((1, D)),
            rows,
            pl.BlockSpec((BLK, 1), lambda i: (at(i), 0)),
        ],
        out_specs=[whole((CELLS, D)), whole((HALO, D)), whole((HALO, D))],
        out_shape=[jax.ShapeDtypeStruct((CELLS, D), bf16), rim, rim],
        scratch_shapes=[pltpu.VMEM((BLK, D), f32), pltpu.VMEM((BLK, D), f32)],
        compiler_params=pltpu.CompilerParams(vmem_limit_bytes=VMEM_LIMIT),
        cost_estimate=pl.CostEstimate(
            flops=4 * CELLS * D * D, bytes_accessed=10 << 20, transcendentals=0
        ),
        name="latent",
    )(edges, g, w_out, d_pre, w_mix, gain, normed, inverse)


def rim_kernel(grad_ref, near_ref, far_ref, out_ref):
    first_core = lax.rem(lax.axis_index("space"), 2) == 0
    other = jnp.where((pl.program_id(0) == 0) == first_core, far_ref[...], near_ref[...])
    out_ref[...] = (grad_ref[...].astype(f32) + other.astype(f32)).astype(bf16)


def add_rims(grad, near, far):
    rim = pl.BlockSpec((HALO, D), lambda i: (i * (CELLS // HALO - 1), 0))
    return pl.pallas_call(
        rim_kernel,
        grid=(2,),
        in_specs=[rim, whole((HALO, D)), whole((HALO, D))],
        out_specs=rim,
        out_shape=jax.ShapeDtypeStruct((CELLS, D), bf16),
        input_output_aliases={0: 0},
        compiler_params=pltpu.CompilerParams(vmem_limit_bytes=VMEM_LIMIT),
        cost_estimate=pl.CostEstimate(flops=1 << 18, bytes_accessed=3 << 19, transcendentals=0),
        name="rims",
    )(grad, near, far)


def along(value, axis, move):
    pairs = [(i, move(i)) for i in range(lax.axis_size(axis))]
    return lax.ppermute(value, axis, [pair for pair in pairs if pair[1] is not None])


def other_core(i):
    return i ^ 1


def other_chip(i):
    there = i + 1 if i % 2 else i - 1
    return there if 0 <= there < 32 else None


def summed(parts):
    total = parts[0].astype(f32)
    for part in parts[1:]:
        total = total + part.astype(f32)
    return total


def shards(latent, neighbours, norm_gain, w_mix, w_out, observed, cell_area, var_weight):
    space = lax.axis_index("space")
    pos = jnp.stack([space // 8, space // 2 % 4, space % 2]).astype(jnp.int32)
    center = latent[0]
    first_core = space % 2 == 0
    head, tail = center[:HALO], center[CELLS - HALO :]
    far = along(jnp.where(first_core, head, tail), "space", other_chip)
    near = along(jnp.where(first_core, tail, head), "space", other_core)
    gain = norm_gain.reshape(1, D)
    area = cell_area.reshape(1, CELLS)
    observed = jnp.pad(observed, ((0, ROWS - VARS), (0, 0)))
    weight = jnp.pad(var_weight, (0, ROWS - VARS)).reshape(ROWS, 1)

    out_t, mix, arrays = forward(neighbours, center, near, far, gain, w_mix, w_out.T)
    edges, normed, hidden, deriv, inverse, pred, pieces = arrays
    pieces = lax.all_to_all(pieces, "member", 0, 0, tiled=True)
    pairs = pair_terms(pieces, observed, area, weight)
    pairs = lax.all_to_all(pairs, "member", 0, 0, tiled=True)
    g, d_pre, losses, keep, send = weight_parts(
        pos, pairs, pred, observed, area, weight, out_t, deriv, hidden, normed
    )
    got = along(send, "space", other_core)

    def over_x(k):
        return along(summed([keep[k], got[k]]).astype(bf16), "space", lambda i: (i + 8 * k) % 32)

    arrived = [over_x(k) for k in (1, 2, 3)]
    grad, near, far = latent_parts(edges, g, out_t, d_pre, w_mix, gain, normed, inverse)
    arrived, grad = lax.optimization_barrier((arrived, grad))
    far = along(far, "space", other_chip)
    near = along(near, "space", other_core)
    share = summed([keep[0], got[0]] + arrived).astype(bf16)

    def over_z(k):
        return along(share[k], "space", lambda i: i // 8 * 8 + (i + 2 * k) % 8)

    arrived = [over_z(k) for k in (1, 2, 3)]
    arrived, near, far = lax.optimization_barrier((arrived, near, far))
    share = summed([share[0]] + arrived).astype(bf16)
    arrived = [along(share, "member", lambda i: (i + 2 * k) % 8) for k in (1, 2, 3)]
    grad = add_rims(grad, near, far)
    arrived, grad = lax.optimization_barrier((arrived, grad))
    share = summed([share] + arrived).astype(bf16)
    totals = summed([share, along(share, "member", lambda i: i ^ 1)])
    grad_scale = 1.0 / math.sqrt(MEMBERS * CELLS * 32)
    return (
        losses.reshape(CELLS),
        grad[None],
        totals[:, :D] * grad_scale,
        totals[:, D : D + VARS] * grad_scale,
    )


def solution(mesh):
    return jax.shard_map(
        shards,
        mesh=mesh,
        in_specs=(
            P("member", "space", None),
            P(None, "space"),
            P(),
            P(),
            P(),
            P(None, "space"),
            P("space"),
            P(),
        ),
        out_specs=(P("space"), P("member", "space", None), P("space", None), P("space", None)),
        check_vma=False,
    )
```

```python
import math

import jax
import jax.numpy as jnp
from jax import lax
from jax.experimental import pallas as pl
from jax.experimental.pallas import tpu as pltpu
from jax.sharding import PartitionSpec as P

D = 1024
VARS = 100
NBRS = 4
HALO = 128
ROWS = 112
MEMBERS = 8
CELLS = 1024
BLK = 256
STEPS = CELLS // BLK
PIECE = CELLS // MEMBERS
WIDE = D + 128

smoothing = 0.1
root_two_pi = math.sqrt(2.0 / math.pi)
cubic = 0.044715
epsilon = 1e-06
fair_shift = 0.05
fair_weight = 1.0 - fair_shift / MEMBERS
pair_coef = fair_weight / (2.0 * MEMBERS * (MEMBERS - 1))

bf16 = jnp.bfloat16
f32 = jnp.float32
VMEM_LIMIT = 24 * 1024 * 1024


def whole(shape):
    return pl.BlockSpec(shape, lambda *_: (0,) * len(shape), pipeline_mode=pl.Buffered(1))


def edge_matrix(neighbours, base, width):
    local = (neighbours - base).T
    shape = (local.shape[0], width)
    column = lax.broadcasted_iota(jnp.int32, shape, 1)
    row = lax.broadcasted_iota(jnp.int32, shape, 0)
    count = jnp.where(column == row + HALO, float(NBRS), 0.0)
    for k in range(NBRS):
        count = count + jnp.where(column == local[:, k : k + 1], 1.0, 0.0)
    return count.astype(bf16)


def gathered(edges, window):
    return jnp.dot(edges, window, preferred_element_type=f32) * (1.0 / NBRS)


def decode(combined, gain, mix, out_t, normed_ref, hidden_ref, deriv_ref, inv_ref, pred_ref, send_ref):
    inverse = lax.rsqrt(jnp.mean(combined * combined, axis=1, keepdims=True) + epsilon)
    normed = (combined * inverse * gain).astype(bf16)
    normed_ref[...] = normed
    inv_ref[...] = inverse
    x = jnp.dot(normed, mix, preferred_element_type=f32)
    square = x * x
    tanh = jnp.tanh(x * (root_two_pi + (root_two_pi * cubic) * square))
    half = 0.5 + 0.5 * tanh
    activation = x * half
    deriv_ref[...] = (
        half + activation * (1.0 - tanh) * (root_two_pi + (3.0 * root_two_pi * cubic) * square)
    ).astype(bf16)
    hidden = (combined + activation).astype(bf16)
    hidden_ref[...] = hidden
    pred = lax.dot_general(out_t, hidden, (((1,), (1,)), ((), ())), preferred_element_type=f32)
    pred_ref[...] = pred
    rounded = pred.astype(bf16)
    for j in range(BLK // PIECE):
        send_ref[j] = rounded[:, j * PIECE : (j + 1) * PIECE]


def interior_kernel(
    nb0_ref, nb1_ref, gain_ref, out_ref, lat_hbm, mix_hbm,
    out_t_ref, ends_ref, mix_out, edges_ref, normed_ref, hidden_ref, deriv_ref, inv_ref, pred_ref,
    *refs,
):
    send_ref, lat, mix, sems = refs
    step = pl.program_id(0)
    copies = [
        pltpu.make_async_copy(
            lat_hbm.at[i * BLK : (i + 1) * BLK], lat.at[i * BLK : (i + 1) * BLK], sems.at[i]
        )
        for i in range(STEPS)
    ] + [
        pltpu.make_async_copy(
            mix_hbm.at[i * BLK : (i + 1) * BLK], mix.at[i * BLK : (i + 1) * BLK], sems.at[STEPS + i]
        )
        for i in range(STEPS)
    ]
    first = pl.multiple_of(step * BLK, BLK)

    @pl.when(step == 0)
    def _():
        for at in (0, 1, 4, 5, 6, 7, 2, 3):
            copies[at].start()
        row = lax.broadcasted_iota(jnp.int32, (ROWS, VARS), 0)
        column = lax.broadcasted_iota(jnp.int32, (ROWS, VARS), 1)
        pick = jnp.where(row == column, 1.0, 0.0).astype(bf16)
        out_t_ref[...] = lax.dot_general(
            pick, out_ref[...], (((1,), (0,)), ((), ())), preferred_element_type=f32
        ).astype(bf16)

    neighbours = jnp.concatenate([nb0_ref[...], nb1_ref[...]], axis=1)
    base = lax.axis_index("space") * CELLS + first
    edges = edge_matrix(neighbours, base, BLK + 2 * HALO)
    edges_ref[...] = edges

    @pl.when(step == 0)
    def _():
        for copy in copies[0:2] + copies[STEPS:]:
            copy.wait()

    @pl.when(step == 1)
    def _():
        copies[2].wait()

    @pl.when(step == 2)
    def _():
        copies[3].wait()

    combined = gathered(edges, lat[pl.ds(first, BLK + 2 * HALO)])
    decode(
        combined, gain_ref[...], mix[...], out_t_ref[...],
        normed_ref, hidden_ref, deriv_ref, inv_ref, pred_ref, send_ref,
    )

    @pl.when(step == STEPS - 2)
    def _():
        ends_ref[0:BLK] = lat[0:BLK]
        ends_ref[BLK:] = lat[CELLS - BLK :]
        mix_out[...] = mix[...]


def rim_cells_kernel(
    nb0_ref, nb1_ref, ends_ref, near_ref, far_ref, gain_ref, mix_ref, out_t_ref,
    *refs,
):
    edges_ref, *refs = refs[len(refs) // 2 :]
    space = lax.axis_index("space")
    start = space * CELLS
    first_core = lax.rem(space, 2) == 0
    low = jnp.where(first_core, far_ref[...], near_ref[...])
    high = jnp.where(first_core, near_ref[...], far_ref[...])
    last_edges = edge_matrix(nb0_ref[...], start + CELLS - BLK, BLK + HALO)
    head_edges = edge_matrix(nb1_ref[...], start - HALO, BLK + HALO)
    edges_ref[0:HALO, 0 : BLK + HALO] = last_edges
    edges_ref[HALO:, 0 : BLK + HALO] = head_edges
    last = gathered(last_edges, jnp.concatenate([ends_ref[BLK:], high], axis=0))
    head = gathered(head_edges, jnp.concatenate([low, ends_ref[0:BLK]], axis=0))
    combined = jnp.concatenate([last, head], axis=0)
    decode(combined, gain_ref[...], mix_ref[...], out_t_ref[...], *refs)


def in_hbm(value):
    return pltpu.with_memory_space_constraint(value, pltpu.HBM)


def forward(neighbours, center, near, far, gain, w_mix, w_out):
    shapes = [
        pltpu.HBM((CELLS, BLK + 2 * HALO), bf16),
        pltpu.HBM((CELLS, D), bf16),
        pltpu.HBM((CELLS, D), bf16),
        pltpu.HBM((CELLS, D), bf16),
        pltpu.HBM((CELLS, 1), f32),
        pltpu.HBM((ROWS, CELLS), f32),
        pltpu.HBM((MEMBERS, ROWS, PIECE), bf16),
    ]

    def blocks(at):
        rows = pl.BlockSpec((BLK, D), lambda i: (at(i), 0))
        return [
            pl.BlockSpec((BLK, BLK + 2 * HALO), lambda i: (at(i), 0)),
            rows,
            rows,
            rows,
            pl.BlockSpec((BLK, 1), lambda i: (at(i), 0)),
            pl.BlockSpec((ROWS, BLK), lambda i: (0, at(i))),
            pl.BlockSpec((BLK // PIECE, ROWS, PIECE), lambda i: (at(i), 0, 0)),
        ]

    def edges_at(column):
        return pl.BlockSpec((NBRS, PIECE), lambda i: (0, column(i)))

    def cost(steps):
        return pl.CostEstimate(
            flops=steps * 4 * BLK * D * D, bytes_accessed=steps * 3 << 20, transcendentals=steps * BLK * D
        )

    neighbours, gain = in_hbm(neighbours), in_hbm(gain)
    out_t, ends, mix, *arrays = pl.pallas_call(
        interior_kernel,
        grid=(STEPS - 1,),
        in_specs=[
            edges_at(lambda i: 2 * i + 1),
            edges_at(lambda i: 2 * i + 2),
            whole((1, D)),
            whole((VARS, D)),
            pl.BlockSpec(memory_space=pltpu.HBM),
            pl.BlockSpec(memory_space=pltpu.HBM),
        ],
        out_specs=[whole((ROWS, D)), whole((2 * BLK, D)), whole((D, D))] + blocks(lambda i: i),
        out_shape=[
            jax.ShapeDtypeStruct((ROWS, D), bf16),
            jax.ShapeDtypeStruct((2 * BLK, D), bf16),
            jax.ShapeDtypeStruct((D, D), bf16),
        ]
        + shapes,
        scratch_shapes=[
            pltpu.VMEM((CELLS, D), bf16),
            pltpu.VMEM((D, D), bf16),
            pltpu.SemaphoreType.DMA((2 * STEPS,)),
        ],
        compiler_params=pltpu.CompilerParams(vmem_limit_bytes=VMEM_LIMIT),
        cost_estimate=cost(STEPS - 1),
        name="interior",
    )(neighbours, neighbours, gain, in_hbm(w_out), in_hbm(center), in_hbm(w_mix))
    arrays = pl.pallas_call(
        rim_cells_kernel,
        grid=(1,),
        in_specs=[
            edges_at(lambda i: MEMBERS - 1),
            edges_at(lambda i: 0),
            whole((2 * BLK, D)),
            whole((HALO, D)),
            whole((HALO, D)),
            whole((1, D)),
            whole((D, D)),
            whole((ROWS, D)),
        ]
        + [pl.BlockSpec(memory_space=pltpu.HBM)] * len(shapes),
        out_specs=blocks(lambda i: STEPS - 1),
        out_shape=shapes,
        input_output_aliases={8 + i: i for i in range(len(shapes))},
        compiler_params=pltpu.CompilerParams(vmem_limit_bytes=VMEM_LIMIT),
        cost_estimate=cost(1),
        name="rim_cells",
    )(neighbours, neighbours, ends, near, far, gain, mix, out_t, *arrays)
    return out_t, mix, arrays


def pair_kernel(pred_ref, obs_ref, area_ref, weight_ref, back_ref):
    area = area_ref[...]
    loss = jnp.zeros((16, PIECE), f32)
    for tile in range(ROWS // 16):
        rows = slice(16 * tile, 16 * tile + 16)
        preds = [pred_ref[m, rows].astype(f32) for m in range(MEMBERS)]
        observed = obs_ref[rows]
        slopes = [jnp.zeros((16, PIECE), f32)] * MEMBERS
        near = jnp.zeros((16, PIECE), f32)
        apart = jnp.zeros((16, PIECE), f32)
        for m in range(MEMBERS):
            gap = preds[m] - observed
            value = gap * gap + smoothing * smoothing
            near = near + value * lax.rsqrt(value)
            for k in range(m + 1, MEMBERS):
                gap = preds[m] - preds[k]
                value = gap * gap + smoothing * smoothing
                root = lax.rsqrt(value)
                apart = apart + value * root
                slope = gap * root
                slopes[m] = slopes[m] + slope
                slopes[k] = slopes[k] - slope
        loss = loss + weight_ref[rows] * (
            near * (1.0 / MEMBERS) - (2.0 * pair_coef) * apart
        )
        if tile < ROWS // 16 - 1:
            for m in range(MEMBERS):
                back_ref[m, rows] = slopes[m].astype(bf16)
    loss = jnp.sum(loss, axis=0, keepdims=True) * area
    high = loss.astype(bf16).astype(f32)
    middle = (loss - high).astype(bf16).astype(f32)
    low = loss - high - middle
    row = lax.broadcasted_iota(jnp.int32, (16, PIECE), 0) - (VARS - (ROWS - 16))
    for m in range(MEMBERS):
        tail = jnp.where(row < 0, slopes[m], 0.0)
        for at, part in enumerate((high, middle, low)):
            tail = jnp.where(row == at, part, tail)
        back_ref[m, ROWS - 16 : ROWS] = tail.astype(bf16)


def pair_terms(preds, observed, area, weight):
    column = lambda i: (0, lax.rem(lax.axis_index("member") + 1, MEMBERS))
    return pl.pallas_call(
        pair_kernel,
        grid=(1,),
        in_specs=[
            whole((MEMBERS, ROWS, PIECE)),
            pl.BlockSpec((ROWS, PIECE), column),
            pl.BlockSpec((1, PIECE), column),
            whole((ROWS, 1)),
        ],
        out_specs=whole((MEMBERS, ROWS, PIECE)),
        out_shape=pltpu.HBM((MEMBERS, ROWS, PIECE), bf16),
        cost_estimate=pl.CostEstimate(
            flops=1 << 24, bytes_accessed=1 << 20, transcendentals=1 << 20
        ),
        compiler_params=pltpu.CompilerParams(vmem_limit_bytes=VMEM_LIMIT),
        name="pairs",
    )(preds, in_hbm(observed), area, weight)


def weights_kernel(
    pos_ref, pair_ref, pred_ref, obs0_ref, obs1_ref, area0_ref, area1_ref, weight_ref, out_ref, deriv_ref, hidden_ref, normed_ref,
    g_ref, pre_ref, loss_ref, keep_ref, send_ref, pre_all, g_all,
):
    step = pl.program_id(0)

    @pl.when(step < STEPS)
    def _():
        pair = jnp.concatenate([pair_ref[j] for j in range(BLK // PIECE)], axis=1).astype(f32)
        loss = jnp.sum(pair[VARS : VARS + 3], axis=0, keepdims=True)
        for j in range(BLK // PIECE):
            at = lax.rem(2 * step + 1 + j, MEMBERS) * PIECE
            loss_ref[:, pl.ds(pl.multiple_of(at, PIECE), PIECE)] = loss[:, j * PIECE : (j + 1) * PIECE]
        area = jnp.concatenate([area0_ref[...], area1_ref[...]], axis=1)
        gap = pred_ref[...] - jnp.concatenate([obs0_ref[...], obs1_ref[...]], axis=1)
        slope = gap * lax.rsqrt(gap * gap + smoothing * smoothing)
        g = (
            weight_ref[...]
            * area
            * (slope * (1.0 / MEMBERS) - (2.0 * pair_coef) * pair)
        ).astype(bf16)
        g_ref[...] = g
        d_hidden = lax.dot_general(
            g, out_ref[...], (((0,), (0,)), ((), ())), preferred_element_type=f32
        )
        d_pre = (d_hidden * deriv_ref[...].astype(f32)).astype(bf16)
        pre_ref[...] = d_pre
        rows = pl.ds(pl.multiple_of(step * BLK, BLK), BLK)
        pre_all[rows] = d_pre
        g_all[:, rows] = g

    @pl.when(step >= STEPS)
    def _():
        mix = lax.dot_general(
            normed_ref[...], pre_all[...], (((0,), (0,)), ((), ())), preferred_element_type=f32
        ).astype(bf16)
        out = jnp.dot(g_all[...], hidden_ref[...], preferred_element_type=f32)
        out = jnp.concatenate([out, jnp.zeros((128 - ROWS, BLK), f32)], axis=0).T.astype(bf16)
        mine = pos_ref[2] == 0
        for z in range(4):
            at = lax.rem(z + 4 - pos_ref[1], 4)
            for source, lanes in ((mix, slice(0, D)), (out, slice(D, WIDE))):
                even = source[64 * z : 64 * z + 32]
                odd = source[64 * z + 32 : 64 * z + 64]
                keep_ref[0, at, :, lanes] = jnp.where(mine, even, odd)
                send_ref[0, at, :, lanes] = jnp.where(mine, odd, even)


def weight_parts(pos, pair, pred, observed, area, weight, w_out, deriv, hidden, normed):
    first = lambda i: jnp.minimum(i, STEPS - 1)
    later = lambda i: jnp.maximum(i - STEPS, 0)
    rows = pl.BlockSpec((BLK, D), lambda i, pos: (first(i), 0))
    columns = pl.BlockSpec((ROWS, BLK), lambda i, pos: (0, first(i)))
    features = pl.BlockSpec((CELLS, BLK), lambda i, pos: (0, lax.rem(pos[0] + later(i), 4)))
    left = lambda i, pos: (0, 2 * first(i) + 1)
    right = lambda i, pos: (0, lax.rem(2 * first(i) + 2, MEMBERS))
    share = pl.BlockSpec((1, 4, 32, WIDE), lambda i, pos: (later(i), 0, 0, 0))
    return pl.pallas_call(
        weights_kernel,
        grid_spec=pltpu.PrefetchScalarGridSpec(
            num_scalar_prefetch=1,
            grid=(2 * STEPS,),
            in_specs=[
                pl.BlockSpec((BLK // PIECE, ROWS, PIECE), lambda i, pos: (first(i), 0, 0)),
                columns,
                pl.BlockSpec((ROWS, PIECE), left),
                pl.BlockSpec((ROWS, PIECE), right),
                pl.BlockSpec((1, PIECE), left),
                pl.BlockSpec((1, PIECE), right),
                whole((ROWS, 1)),
                whole((ROWS, D)),
                rows,
                features,
                features,
            ],
            out_specs=[columns, rows, whole((1, CELLS)), share, share],
            scratch_shapes=[pltpu.VMEM((CELLS, D), bf16), pltpu.VMEM((ROWS, CELLS), bf16)],
        ),
        out_shape=[
            jax.ShapeDtypeStruct((ROWS, CELLS), bf16),
            jax.ShapeDtypeStruct((CELLS, D), bf16),
            jax.ShapeDtypeStruct((1, CELLS), f32),
            jax.ShapeDtypeStruct((4, 4, 32, WIDE), bf16),
            jax.ShapeDtypeStruct((4, 4, 32, WIDE), bf16),
        ],
        compiler_params=pltpu.CompilerParams(vmem_limit_bytes=VMEM_LIMIT),
        cost_estimate=pl.CostEstimate(
            flops=3 * CELLS * D * D, bytes_accessed=14 << 20, transcendentals=0
        ),
        name="weights",
    )(
        pos, pair, in_hbm(pred), in_hbm(observed), in_hbm(observed), area, area, weight, w_out,
        in_hbm(deriv), in_hbm(hidden), in_hbm(normed),
    )


def latent_kernel(
    edges_ref, g_ref, out_ref, pre_ref, mix_ref, gain_ref, normed_ref, inv_ref,
    grad_ref, near_ref, far_ref, carry, tail,
):
    step = pl.program_id(0)
    d_hidden = lax.dot_general(
        g_ref[...], out_ref[...], (((0,), (0,)), ((), ())), preferred_element_type=f32
    )
    d_normed = lax.dot_general(
        pre_ref[...], mix_ref[...], (((1,), (1,)), ((), ())), preferred_element_type=f32
    )
    gain = gain_ref[...]
    normed = normed_ref[...].astype(f32)
    mean = jnp.mean(normed * d_normed, axis=1, keepdims=True)
    d_combined = d_hidden + inv_ref[...] * (d_normed * gain - normed * (1.0 / gain) * mean)
    d_combined = d_combined.astype(bf16)

    def spread(edges, cells):
        return (1.0 / NBRS) * lax.dot_general(
            edges, cells, (((0,), (0,)), ((), ())), preferred_element_type=f32
        )

    @pl.when(step == 0)
    def _():
        last = spread(edges_ref[0:HALO, 0 : BLK + HALO], d_combined[0:HALO])
        tail[...] = last[0:BLK]
        head = spread(edges_ref[HALO:, 0 : BLK + HALO], d_combined[HALO:])
        carry[...] = head[HALO:]
        high, low = last[BLK:].astype(bf16), head[0:HALO].astype(bf16)
        first_core = lax.rem(lax.axis_index("space"), 2) == 0
        near_ref[...] = jnp.where(first_core, high, low)
        far_ref[...] = jnp.where(first_core, low, high)

    @pl.when(step > 0)
    def _():
        first = pl.multiple_of((step - 1) * BLK, BLK)
        part = spread(edges_ref[...], d_combined)
        grad_ref[pl.ds(first, BLK)] = (part[0:BLK] + carry[...]).astype(bf16)
        carry[...] = part[BLK:]

    @pl.when(step == STEPS - 1)
    def _():
        grad_ref[CELLS - BLK :] = (carry[...] + tail[...]).astype(bf16)


def latent_parts(edges, g, w_out, d_pre, w_mix, gain, normed, inverse):
    at = lambda i: lax.rem(i + STEPS - 1, STEPS)
    rows = pl.BlockSpec((BLK, D), lambda i: (at(i), 0))
    rim = jax.ShapeDtypeStruct((HALO, D), bf16)
    return pl.pallas_call(
        latent_kernel,
        grid=(STEPS,),
        in_specs=[
            pl.BlockSpec((BLK, BLK + 2 * HALO), lambda i: (at(i), 0)),
            pl.BlockSpec((ROWS, BLK), lambda i: (0, at(i))),
            whole((ROWS, D)),
            rows,
            whole((D, D)),
            whole((1, D)),
            rows,
            pl.BlockSpec((BLK, 1), lambda i: (at(i), 0)),
        ],
        out_specs=[whole((CELLS, D)), whole((HALO, D)), whole((HALO, D))],
        out_shape=[jax.ShapeDtypeStruct((CELLS, D), bf16), rim, rim],
        scratch_shapes=[pltpu.VMEM((BLK, D), f32), pltpu.VMEM((BLK, D), f32)],
        compiler_params=pltpu.CompilerParams(vmem_limit_bytes=VMEM_LIMIT),
        cost_estimate=pl.CostEstimate(
            flops=4 * CELLS * D * D, bytes_accessed=10 << 20, transcendentals=0
        ),
        name="latent",
    )(edges, g, w_out, d_pre, w_mix, gain, normed, inverse)


def rim_kernel(grad_ref, near_ref, far_ref, out_ref):
    first_core = lax.rem(lax.axis_index("space"), 2) == 0
    other = jnp.where((pl.program_id(0) == 0) == first_core, far_ref[...], near_ref[...])
    out_ref[...] = (grad_ref[...].astype(f32) + other.astype(f32)).astype(bf16)


def add_rims(grad, near, far):
    rim = pl.BlockSpec((HALO, D), lambda i: (i * (CELLS // HALO - 1), 0))
    return pl.pallas_call(
        rim_kernel,
        grid=(2,),
        in_specs=[rim, whole((HALO, D)), whole((HALO, D))],
        out_specs=rim,
        out_shape=jax.ShapeDtypeStruct((CELLS, D), bf16),
        input_output_aliases={0: 0},
        compiler_params=pltpu.CompilerParams(vmem_limit_bytes=VMEM_LIMIT),
        cost_estimate=pl.CostEstimate(flops=1 << 18, bytes_accessed=3 << 19, transcendentals=0),
        name="rims",
    )(grad, near, far)


def along(value, axis, move):
    pairs = [(i, move(i)) for i in range(lax.axis_size(axis))]
    return lax.ppermute(value, axis, [pair for pair in pairs if pair[1] is not None])


def other_core(i):
    return i ^ 1


def other_chip(i):
    there = i + 1 if i % 2 else i - 1
    return there if 0 <= there < 32 else None


def summed(parts):
    total = parts[0].astype(f32)
    for part in parts[1:]:
        total = total + part.astype(f32)
    return total


def shards(latent, neighbours, norm_gain, w_mix, w_out, observed, cell_area, var_weight):
    space = lax.axis_index("space")
    pos = jnp.stack([space // 8, space // 2 % 4, space % 2]).astype(jnp.int32)
    center = latent[0]
    first_core = space % 2 == 0
    head, tail = center[:HALO], center[CELLS - HALO :]
    far = along(jnp.where(first_core, head, tail), "space", other_chip)
    near = along(jnp.where(first_core, tail, head), "space", other_core)
    gain = norm_gain.reshape(1, D)
    area = cell_area.reshape(1, CELLS)
    observed = jnp.pad(observed, ((0, ROWS - VARS), (0, 0)))
    weight = jnp.pad(var_weight, (0, ROWS - VARS)).reshape(ROWS, 1)

    out_t, mix, arrays = forward(neighbours, center, near, far, gain, w_mix, w_out.T)
    edges, normed, hidden, deriv, inverse, pred, pieces = arrays
    pieces = lax.all_to_all(pieces, "member", 0, 0, tiled=True)
    pairs = pair_terms(pieces, observed, area, weight)
    pairs = lax.all_to_all(pairs, "member", 0, 0, tiled=True)
    g, d_pre, losses, keep, send = weight_parts(
        pos, pairs, pred, observed, area, weight, out_t, deriv, hidden, normed
    )
    got = along(send, "space", other_core)

    def over_x(k):
        return along(summed([keep[k], got[k]]).astype(bf16), "space", lambda i: (i + 8 * k) % 32)

    arrived = [over_x(k) for k in (1, 2, 3)]
    grad, near, far = latent_parts(edges, g, out_t, d_pre, w_mix, gain, normed, inverse)
    arrived, grad = lax.optimization_barrier((arrived, grad))
    far = along(far, "space", other_chip)
    near = along(near, "space", other_core)
    share = summed([keep[0], got[0]] + arrived).astype(bf16)

    def over_z(k):
        return along(share[k], "space", lambda i: i // 8 * 8 + (i + 2 * k) % 8)

    share = summed([share[0]] + [over_z(k) for k in (1, 2, 3)]).astype(bf16)
    arrived = [along(share, "member", lambda i: (i + 2 * k) % 8) for k in (1, 2, 3)]
    arrived, near, far = lax.optimization_barrier((arrived, near, far))
    share = summed([share] + arrived).astype(bf16)
    totals = summed([share, along(share, "member", lambda i: i ^ 1)])
    grad = add_rims(grad, near, far)
    grad_scale = 1.0 / math.sqrt(MEMBERS * CELLS * 32)
    return (
        losses.reshape(CELLS),
        grad[None],
        totals[:, :D] * grad_scale,
        totals[:, D : D + VARS] * grad_scale,
    )


def solution(mesh):
    return jax.shard_map(
        shards,
        mesh=mesh,
        in_specs=(
            P("member", "space", None),
            P(None, "space"),
            P(),
            P(),
            P(),
            P(None, "space"),
            P("space"),
            P(),
        ),
        out_specs=(P("space"), P("member", "space", None), P("space", None), P("space", None)),
        check_vma=False,
    )
```

```python
import math

import jax
import jax.numpy as jnp
from jax import lax
from jax.experimental import pallas as pl
from jax.experimental.pallas import tpu as pltpu
from jax.sharding import PartitionSpec as P

D = 1024
VARS = 100
NBRS = 4
HALO = 128
ROWS = 112
MEMBERS = 8
CELLS = 1024
BLK = 256
STEPS = CELLS // BLK
PIECE = CELLS // MEMBERS
WIDE = D + 128

smoothing = 0.1
root_two_pi = math.sqrt(2.0 / math.pi)
cubic = 0.044715
epsilon = 1e-06
fair_shift = 0.05
fair_weight = 1.0 - fair_shift / MEMBERS
pair_coef = fair_weight / (2.0 * MEMBERS * (MEMBERS - 1))

bf16 = jnp.bfloat16
f32 = jnp.float32
VMEM_LIMIT = 24 * 1024 * 1024


def whole(shape):
    return pl.BlockSpec(shape, lambda *_: (0,) * len(shape), pipeline_mode=pl.Buffered(1))


def edge_matrix(neighbours, base, width):
    local = (neighbours - base).T
    shape = (local.shape[0], width)
    column = lax.broadcasted_iota(jnp.int32, shape, 1)
    row = lax.broadcasted_iota(jnp.int32, shape, 0)
    count = jnp.where(column == row + HALO, float(NBRS), 0.0)
    for k in range(NBRS):
        count = count + jnp.where(column == local[:, k : k + 1], 1.0, 0.0)
    return count.astype(bf16)


def gathered(edges, window):
    return jnp.dot(edges, window, preferred_element_type=f32) * (1.0 / NBRS)


def decode(combined, gain, mix, out_t, normed_ref, hidden_ref, deriv_ref, inv_ref, pred_ref, send_ref):
    inverse = lax.rsqrt(jnp.mean(combined * combined, axis=1, keepdims=True) + epsilon)
    normed = (combined * inverse * gain).astype(bf16)
    normed_ref[...] = normed
    inv_ref[...] = inverse
    x = jnp.dot(normed, mix(), preferred_element_type=f32)
    square = x * x
    tanh = jnp.tanh(x * (root_two_pi + (root_two_pi * cubic) * square))
    half = 0.5 + 0.5 * tanh
    activation = x * half
    deriv_ref[...] = (
        half + activation * (1.0 - tanh) * (root_two_pi + (3.0 * root_two_pi * cubic) * square)
    ).astype(bf16)
    hidden = (combined + activation).astype(bf16)
    hidden_ref[...] = hidden
    pred = lax.dot_general(out_t, hidden, (((1,), (1,)), ((), ())), preferred_element_type=f32)
    pred_ref[...] = pred
    rounded = pred.astype(bf16)
    for j in range(BLK // PIECE):
        send_ref[j] = rounded[:, j * PIECE : (j + 1) * PIECE]


def interior_kernel(
    nb0_ref, nb1_ref, gain_ref, out_ref, lat_hbm, mix_hbm,
    out_t_ref, lat, mix, normed_ref, hidden_ref, deriv_ref, inv_ref, pred_ref,
    *refs,
):
    send_ref, sems = refs
    step = pl.program_id(0)
    copies = [
        pltpu.make_async_copy(
            lat_hbm.at[i * BLK : (i + 1) * BLK], lat.at[i * BLK : (i + 1) * BLK], sems.at[i]
        )
        for i in range(STEPS)
    ] + [
        pltpu.make_async_copy(
            mix_hbm.at[i * BLK : (i + 1) * BLK], mix.at[i * BLK : (i + 1) * BLK], sems.at[STEPS + i]
        )
        for i in range(STEPS)
    ]
    first = pl.multiple_of(step * BLK, BLK)

    @pl.when(step == 0)
    def _():
        for at in (0, 1, 4, 5, 6, 7, 2, 3):
            copies[at].start()
        row = lax.broadcasted_iota(jnp.int32, (ROWS, VARS), 0)
        column = lax.broadcasted_iota(jnp.int32, (ROWS, VARS), 1)
        pick = jnp.where(row == column, 1.0, 0.0).astype(bf16)
        out_t_ref[...] = lax.dot_general(
            pick, out_ref[...], (((1,), (0,)), ((), ())), preferred_element_type=f32
        ).astype(bf16)

    neighbours = jnp.concatenate([nb0_ref[...], nb1_ref[...]], axis=1)
    base = lax.axis_index("space") * CELLS + first
    edges = edge_matrix(neighbours, base, BLK + 2 * HALO)

    @pl.when(step == 0)
    def _():
        for copy in copies[0:2]:
            copy.wait()

    @pl.when(step == 1)
    def _():
        copies[2].wait()

    @pl.when(step == 2)
    def _():
        copies[3].wait()

    def loaded_mix():
        @pl.when(step == 0)
        def _():
            for copy in copies[STEPS:]:
                copy.wait()

        return mix[...]

    combined = gathered(edges, lat[pl.ds(first, BLK + 2 * HALO)])
    decode(
        combined, gain_ref[...], loaded_mix, out_t_ref[...],
        normed_ref, hidden_ref, deriv_ref, inv_ref, pred_ref, send_ref,
    )


def rim_cells_kernel(
    nb0_ref, nb1_ref, lat_ref, near_ref, far_ref, gain_ref, mix_ref, out_t_ref,
    *refs,
):
    refs = refs[len(refs) // 2 :]
    space = lax.axis_index("space")
    start = space * CELLS
    first_core = lax.rem(space, 2) == 0
    low = jnp.where(first_core, far_ref[...], near_ref[...])
    high = jnp.where(first_core, near_ref[...], far_ref[...])
    last_edges = edge_matrix(nb0_ref[...], start + CELLS - BLK, BLK + HALO)
    head_edges = edge_matrix(nb1_ref[...], start - HALO, BLK + HALO)
    last = gathered(last_edges, jnp.concatenate([lat_ref[CELLS - BLK :], high], axis=0))
    head = gathered(head_edges, jnp.concatenate([low, lat_ref[0:BLK]], axis=0))
    combined = jnp.concatenate([last, head], axis=0)
    decode(combined, gain_ref[...], lambda: mix_ref[...], out_t_ref[...], *refs)


def in_hbm(value):
    return pltpu.with_memory_space_constraint(value, pltpu.HBM)


def forward(neighbours, center, near, far, gain, w_mix, w_out):
    shapes = [
        pltpu.HBM((CELLS, D), bf16),
        pltpu.HBM((CELLS, D), bf16),
        pltpu.HBM((CELLS, D), bf16),
        pltpu.HBM((CELLS, 1), f32),
        pltpu.HBM((ROWS, CELLS), f32),
        pltpu.HBM((MEMBERS, ROWS, PIECE), bf16),
    ]

    def blocks(at):
        rows = pl.BlockSpec((BLK, D), lambda i: (at(i), 0))
        return [
            rows,
            rows,
            rows,
            pl.BlockSpec((BLK, 1), lambda i: (at(i), 0)),
            pl.BlockSpec((ROWS, BLK), lambda i: (0, at(i))),
            pl.BlockSpec((BLK // PIECE, ROWS, PIECE), lambda i: (at(i), 0, 0)),
        ]

    def edges_at(column):
        return pl.BlockSpec((NBRS, PIECE), lambda i: (0, column(i)))

    def cost(steps):
        return pl.CostEstimate(
            flops=steps * 4 * BLK * D * D, bytes_accessed=steps * 3 << 20, transcendentals=steps * BLK * D
        )

    neighbours, gain = in_hbm(neighbours), in_hbm(gain)
    out_t, lat, mix, *arrays = pl.pallas_call(
        interior_kernel,
        grid=(STEPS - 1,),
        in_specs=[
            edges_at(lambda i: 2 * i + 1),
            edges_at(lambda i: 2 * i + 2),
            whole((1, D)),
            whole((VARS, D)),
            pl.BlockSpec(memory_space=pltpu.HBM),
            pl.BlockSpec(memory_space=pltpu.HBM),
        ],
        out_specs=[pl.BlockSpec(memory_space=pltpu.VMEM)] * 3 + blocks(lambda i: i),
        out_shape=[
            jax.ShapeDtypeStruct((ROWS, D), bf16),
            jax.ShapeDtypeStruct((CELLS, D), bf16),
            jax.ShapeDtypeStruct((D, D), bf16),
        ]
        + shapes,
        scratch_shapes=[
            pltpu.SemaphoreType.DMA((2 * STEPS,)),
        ],
        compiler_params=pltpu.CompilerParams(vmem_limit_bytes=VMEM_LIMIT),
        cost_estimate=cost(STEPS - 1),
        name="interior",
    )(neighbours, neighbours, gain, in_hbm(w_out), in_hbm(center), in_hbm(w_mix))
    arrays = pl.pallas_call(
        rim_cells_kernel,
        grid=(1,),
        in_specs=[
            edges_at(lambda i: MEMBERS - 1),
            edges_at(lambda i: 0),
            *[pl.BlockSpec(memory_space=pltpu.VMEM)] * 3,
            whole((1, D)),
            *[pl.BlockSpec(memory_space=pltpu.VMEM)] * 2,
        ]
        + [pl.BlockSpec(memory_space=pltpu.HBM)] * len(shapes),
        out_specs=blocks(lambda i: STEPS - 1),
        out_shape=shapes,
        input_output_aliases={8 + i: i for i in range(len(shapes))},
        compiler_params=pltpu.CompilerParams(vmem_limit_bytes=VMEM_LIMIT),
        cost_estimate=cost(1),
        name="rim_cells",
    )(neighbours, neighbours, lat, near, far, gain, mix, out_t, *arrays)
    return out_t, mix, arrays


def pair_kernel(pred_ref, obs_ref, area_ref, weight_ref, back_ref):
    area = area_ref[...]
    loss = jnp.zeros((16, PIECE), f32)
    for tile in range(ROWS // 16):
        rows = slice(16 * tile, 16 * tile + 16)
        preds = [pred_ref[m, rows].astype(f32) for m in range(MEMBERS)]
        observed = obs_ref[rows]
        slopes = [jnp.zeros((16, PIECE), f32)] * MEMBERS
        near = jnp.zeros((16, PIECE), f32)
        apart = jnp.zeros((16, PIECE), f32)
        for m in range(MEMBERS):
            gap = preds[m] - observed
            value = gap * gap + smoothing * smoothing
            near = near + value * lax.rsqrt(value)
            for k in range(m + 1, MEMBERS):
                gap = preds[m] - preds[k]
                value = gap * gap + smoothing * smoothing
                root = lax.rsqrt(value)
                apart = apart + value * root
                slope = gap * root
                slopes[m] = slopes[m] + slope
                slopes[k] = slopes[k] - slope
        loss = loss + weight_ref[rows] * (
            near * (1.0 / MEMBERS) - (2.0 * pair_coef) * apart
        )
        if tile < ROWS // 16 - 1:
            for m in range(MEMBERS):
                back_ref[m, rows] = slopes[m].astype(bf16)
    loss = jnp.sum(loss, axis=0, keepdims=True) * area
    high = loss.astype(bf16).astype(f32)
    middle = (loss - high).astype(bf16).astype(f32)
    low = loss - high - middle
    row = lax.broadcasted_iota(jnp.int32, (16, PIECE), 0) - (VARS - (ROWS - 16))
    for m in range(MEMBERS):
        tail = jnp.where(row < 0, slopes[m], 0.0)
        for at, part in enumerate((high, middle, low)):
            tail = jnp.where(row == at, part, tail)
        back_ref[m, ROWS - 16 : ROWS] = tail.astype(bf16)


def pair_terms(preds, observed, area, weight):
    column = lambda i: (0, lax.rem(lax.axis_index("member") + 1, MEMBERS))
    return pl.pallas_call(
        pair_kernel,
        grid=(1,),
        in_specs=[
            whole((MEMBERS, ROWS, PIECE)),
            pl.BlockSpec((ROWS, PIECE), column),
            pl.BlockSpec((1, PIECE), column),
            whole((ROWS, 1)),
        ],
        out_specs=whole((MEMBERS, ROWS, PIECE)),
        out_shape=pltpu.HBM((MEMBERS, ROWS, PIECE), bf16),
        cost_estimate=pl.CostEstimate(
            flops=1 << 24, bytes_accessed=1 << 20, transcendentals=1 << 20
        ),
        compiler_params=pltpu.CompilerParams(vmem_limit_bytes=VMEM_LIMIT),
        name="pairs",
    )(preds, in_hbm(observed), area, weight)


def weights_kernel(
    pos_ref, pair_ref, pred_ref, obs0_ref, obs1_ref, area0_ref, area1_ref, weight_ref, out_ref, deriv_ref,
    hidden0_ref, hidden1_ref, normed0_ref, normed1_ref,
    g_ref, pre_ref, loss_ref, keep_ref, send_ref, pre_all, g_all,
):
    step = pl.program_id(0)

    @pl.when(step < STEPS)
    def _():
        pair = jnp.concatenate([pair_ref[j] for j in range(BLK // PIECE)], axis=1).astype(f32)
        loss = jnp.sum(pair[VARS : VARS + 3], axis=0, keepdims=True)
        for j in range(BLK // PIECE):
            at = lax.rem(2 * step + 1 + j, MEMBERS) * PIECE
            loss_ref[:, pl.ds(pl.multiple_of(at, PIECE), PIECE)] = loss[:, j * PIECE : (j + 1) * PIECE]
        area = jnp.concatenate([area0_ref[...], area1_ref[...]], axis=1)
        gap = pred_ref[...] - jnp.concatenate([obs0_ref[...], obs1_ref[...]], axis=1)
        slope = gap * lax.rsqrt(gap * gap + smoothing * smoothing)
        g = (
            weight_ref[...]
            * area
            * (slope * (1.0 / MEMBERS) - (2.0 * pair_coef) * pair)
        ).astype(bf16)
        g_ref[...] = g
        d_hidden = lax.dot_general(
            g, out_ref[...], (((0,), (0,)), ((), ())), preferred_element_type=f32
        )
        d_pre = (d_hidden * deriv_ref[...].astype(f32)).astype(bf16)
        pre_ref[...] = d_pre
        rows = pl.ds(pl.multiple_of(step * BLK, BLK), BLK)
        pre_all[rows] = d_pre
        g_all[:, rows] = g

    @pl.when(step >= STEPS)
    def _():
        mine = pos_ref[2] == 0
        for x, hidden_ref, normed_ref in ((0, hidden0_ref, normed0_ref), (1, hidden1_ref, normed1_ref)):
            mix = lax.dot_general(
                normed_ref[...], pre_all[...], (((0,), (0,)), ((), ())), preferred_element_type=f32
            ).astype(bf16)
            out = jnp.dot(g_all[...], hidden_ref[...], preferred_element_type=f32)
            out = jnp.concatenate([out, jnp.zeros((128 - ROWS, BLK), f32)], axis=0).T.astype(bf16)
            for z in range(4):
                at = lax.rem(z + 4 - pos_ref[1], 4)
                for source, lanes in ((mix, slice(0, D)), (out, slice(D, WIDE))):
                    even = source[64 * z : 64 * z + 32]
                    odd = source[64 * z + 32 : 64 * z + 64]
                    keep_ref[x, at, :, lanes] = jnp.where(mine, even, odd)
                    send_ref[x, at, :, lanes] = jnp.where(mine, odd, even)


def weight_parts(pos, pair, pred, observed, area, weight, w_out, deriv, hidden, normed):
    first = lambda i: jnp.minimum(i, STEPS - 1)
    later = lambda i: jnp.maximum(i - STEPS, 0)
    rows = pl.BlockSpec((BLK, D), lambda i, pos: (first(i), 0))
    columns = pl.BlockSpec((ROWS, BLK), lambda i, pos: (0, first(i)))
    features = [
        pl.BlockSpec((CELLS, BLK), lambda i, pos, k=k: (0, lax.rem(pos[0] + 2 * later(i) + k, 4)))
        for k in (0, 1)
    ]
    left = lambda i, pos: (0, 2 * first(i) + 1)
    right = lambda i, pos: (0, lax.rem(2 * first(i) + 2, MEMBERS))
    share = pl.BlockSpec((2, 4, 32, WIDE), lambda i, pos: (later(i), 0, 0, 0))
    return pl.pallas_call(
        weights_kernel,
        grid_spec=pltpu.PrefetchScalarGridSpec(
            num_scalar_prefetch=1,
            grid=(STEPS + 2,),
            in_specs=[
                pl.BlockSpec((BLK // PIECE, ROWS, PIECE), lambda i, pos: (first(i), 0, 0)),
                columns,
                pl.BlockSpec((ROWS, PIECE), left),
                pl.BlockSpec((ROWS, PIECE), right),
                pl.BlockSpec((1, PIECE), left),
                pl.BlockSpec((1, PIECE), right),
                whole((ROWS, 1)),
                whole((ROWS, D)),
                rows,
                *features,
                *features,
            ],
            out_specs=[columns, rows, whole((1, CELLS)), share, share],
            scratch_shapes=[pltpu.VMEM((CELLS, D), bf16), pltpu.VMEM((ROWS, CELLS), bf16)],
        ),
        out_shape=[
            jax.ShapeDtypeStruct((ROWS, CELLS), bf16),
            jax.ShapeDtypeStruct((CELLS, D), bf16),
            jax.ShapeDtypeStruct((1, CELLS), f32),
            jax.ShapeDtypeStruct((4, 4, 32, WIDE), bf16),
            jax.ShapeDtypeStruct((4, 4, 32, WIDE), bf16),
        ],
        compiler_params=pltpu.CompilerParams(vmem_limit_bytes=VMEM_LIMIT),
        cost_estimate=pl.CostEstimate(
            flops=3 * CELLS * D * D, bytes_accessed=14 << 20, transcendentals=0
        ),
        name="weights",
    )(
        pos, pair, in_hbm(pred), in_hbm(observed), in_hbm(observed), area, area, weight, w_out,
        in_hbm(deriv), in_hbm(hidden), in_hbm(hidden), in_hbm(normed), in_hbm(normed),
    )


def latent_kernel(
    nb0_ref, nb1_ref, g_ref, out_ref, pre_ref, mix_ref, gain_ref, normed_ref, inv_ref,
    grad_ref, near_ref, far_ref, carry, tail,
):
    step = pl.program_id(0)
    d_hidden = lax.dot_general(
        g_ref[...], out_ref[...], (((0,), (0,)), ((), ())), preferred_element_type=f32
    )
    d_normed = lax.dot_general(
        pre_ref[...], mix_ref[...], (((1,), (1,)), ((), ())), preferred_element_type=f32
    )
    gain = gain_ref[...]
    normed = normed_ref[...].astype(f32)
    mean = jnp.mean(normed * d_normed, axis=1, keepdims=True)
    d_combined = d_hidden + inv_ref[...] * (d_normed * gain - normed * (1.0 / gain) * mean)
    d_combined = d_combined.astype(bf16)

    start = lax.axis_index("space") * CELLS

    def spread(edges, cells):
        return (1.0 / NBRS) * lax.dot_general(
            edges, cells, (((0,), (0,)), ((), ())), preferred_element_type=f32
        )

    @pl.when(step == 0)
    def _():
        edges = edge_matrix(nb0_ref[...], start + CELLS - BLK, BLK + HALO)
        last = spread(edges, d_combined[0:HALO])
        tail[...] = last[0:BLK]
        edges = edge_matrix(nb1_ref[...], start - HALO, BLK + HALO)
        head = spread(edges, d_combined[HALO:])
        carry[...] = head[HALO:]
        high, low = last[BLK:].astype(bf16), head[0:HALO].astype(bf16)
        first_core = lax.rem(lax.axis_index("space"), 2) == 0
        near_ref[...] = jnp.where(first_core, high, low)
        far_ref[...] = jnp.where(first_core, low, high)

    @pl.when(step > 0)
    def _():
        first = pl.multiple_of((step - 1) * BLK, BLK)
        neighbours = jnp.concatenate([nb0_ref[...], nb1_ref[...]], axis=1)
        part = spread(edge_matrix(neighbours, start + first, BLK + 2 * HALO), d_combined)
        grad_ref[pl.ds(first, BLK)] = (part[0:BLK] + carry[...]).astype(bf16)
        carry[...] = part[BLK:]

    @pl.when(step == STEPS - 1)
    def _():
        grad_ref[CELLS - BLK :] = (carry[...] + tail[...]).astype(bf16)


def latent_parts(neighbours, g, w_out, d_pre, w_mix, gain, normed, inverse):
    at = lambda i: lax.rem(i + STEPS - 1, STEPS)
    rows = pl.BlockSpec((BLK, D), lambda i: (at(i), 0))
    rim = jax.ShapeDtypeStruct((HALO, D), bf16)
    return pl.pallas_call(
        latent_kernel,
        grid=(STEPS,),
        in_specs=[
            pl.BlockSpec((NBRS, PIECE), lambda i: (0, 2 * at(i) + 1)),
            pl.BlockSpec((NBRS, PIECE), lambda i: (0, lax.rem(2 * at(i) + 2, MEMBERS))),
            pl.BlockSpec((ROWS, BLK), lambda i: (0, at(i))),
            whole((ROWS, D)),
            rows,
            whole((D, D)),
            whole((1, D)),
            rows,
            pl.BlockSpec((BLK, 1), lambda i: (at(i), 0)),
        ],
        out_specs=[whole((CELLS, D)), whole((HALO, D)), whole((HALO, D))],
        out_shape=[jax.ShapeDtypeStruct((CELLS, D), bf16), rim, rim],
        scratch_shapes=[pltpu.VMEM((BLK, D), f32), pltpu.VMEM((BLK, D), f32)],
        compiler_params=pltpu.CompilerParams(vmem_limit_bytes=VMEM_LIMIT),
        cost_estimate=pl.CostEstimate(
            flops=4 * CELLS * D * D, bytes_accessed=10 << 20, transcendentals=0
        ),
        name="latent",
    )(neighbours, neighbours, g, w_out, d_pre, w_mix, gain, normed, inverse)


def rim_kernel(grad_ref, near_ref, far_ref, out_ref):
    first_core = lax.rem(lax.axis_index("space"), 2) == 0
    other = jnp.where((pl.program_id(0) == 0) == first_core, far_ref[...], near_ref[...])
    out_ref[...] = (grad_ref[...].astype(f32) + other.astype(f32)).astype(bf16)


def add_rims(grad, near, far):
    rim = pl.BlockSpec((HALO, D), lambda i: (i * (CELLS // HALO - 1), 0))
    return pl.pallas_call(
        rim_kernel,
        grid=(2,),
        in_specs=[rim, whole((HALO, D)), whole((HALO, D))],
        out_specs=rim,
        out_shape=jax.ShapeDtypeStruct((CELLS, D), bf16),
        input_output_aliases={0: 0},
        compiler_params=pltpu.CompilerParams(vmem_limit_bytes=VMEM_LIMIT),
        cost_estimate=pl.CostEstimate(flops=1 << 18, bytes_accessed=3 << 19, transcendentals=0),
        name="rims",
    )(grad, near, far)


def along(value, axis, move):
    pairs = [(i, move(i)) for i in range(lax.axis_size(axis))]
    return lax.ppermute(value, axis, [pair for pair in pairs if pair[1] is not None])


def other_core(i):
    return i ^ 1


def other_chip(i):
    there = i + 1 if i % 2 else i - 1
    return there if 0 <= there < 32 else None


def summed(parts):
    total = parts[0].astype(f32)
    for part in parts[1:]:
        total = total + part.astype(f32)
    return total


def shards(latent, neighbours, norm_gain, w_mix, w_out, observed, cell_area, var_weight):
    space = lax.axis_index("space")
    pos = jnp.stack([space // 8, space // 2 % 4, space % 2]).astype(jnp.int32)
    center = latent[0]
    first_core = space % 2 == 0
    head, tail = center[:HALO], center[CELLS - HALO :]
    far = along(jnp.where(first_core, head, tail), "space", other_chip)
    near = along(jnp.where(first_core, tail, head), "space", other_core)
    gain = norm_gain.reshape(1, D)
    area = cell_area.reshape(1, CELLS)
    observed = jnp.pad(observed, ((0, ROWS - VARS), (0, 0)))
    weight = jnp.pad(var_weight, (0, ROWS - VARS)).reshape(ROWS, 1)

    out_t, mix, arrays = forward(neighbours, center, near, far, gain, w_mix, w_out.T)
    normed, hidden, deriv, inverse, pred, pieces = arrays
    pieces = lax.all_to_all(pieces, "member", 0, 0, tiled=True)
    pairs = pair_terms(pieces, observed, area, weight)
    pairs = lax.all_to_all(pairs, "member", 0, 0, tiled=True)
    g, d_pre, losses, keep, send = weight_parts(
        pos, pairs, pred, observed, area, weight, out_t, deriv, hidden, normed
    )
    got = along(send, "space", other_core)

    def own(k):
        return summed([keep[k], got[k]]).astype(bf16)

    def over_x(k, value):
        return along(value, "space", lambda i: (i + 8 * k) % 32)

    arrived = [over_x(k, own(k)) for k in (1, 2, 3)]
    grad, near, far = latent_parts(neighbours, g, out_t, d_pre, w_mix, gain, normed, inverse)
    arrived, grad = lax.optimization_barrier((arrived, grad))
    far = along(far, "space", other_chip)
    near = along(near, "space", other_core)
    share = summed([own(0)] + arrived).astype(bf16)

    def over_z(k):
        return along(share[k], "space", lambda i: i // 8 * 8 + (i + 2 * k) % 8)

    share = summed([share[0]] + [over_z(k) for k in (1, 2, 3)]).astype(bf16)
    arrived = [along(share, "member", lambda i: (i + 2 * k) % 8) for k in (1, 2, 3)]
    arrived, near, far = lax.optimization_barrier((arrived, near, far))
    share = summed([share] + arrived).astype(bf16)
    totals = summed([share, along(share, "member", lambda i: i ^ 1)])
    grad = add_rims(grad, near, far)
    grad_scale = 1.0 / math.sqrt(MEMBERS * CELLS * 32)
    return (
        losses.reshape(CELLS),
        grad[None],
        totals[:, :D] * grad_scale,
        totals[:, D : D + VARS] * grad_scale,
    )


def solution(mesh):
    return jax.shard_map(
        shards,
        mesh=mesh,
        in_specs=(
            P("member", "space", None),
            P(None, "space"),
            P(),
            P(),
            P(),
            P(None, "space"),
            P("space"),
            P(),
        ),
        out_specs=(P("space"), P("member", "space", None), P("space", None), P("space", None)),
        check_vma=False,
    )
```

```python
import math

import jax
import jax.numpy as jnp
from jax import lax
from jax.experimental import pallas as pl
from jax.experimental.pallas import tpu as pltpu
from jax.sharding import PartitionSpec as P

D = 1024
VARS = 100
NBRS = 4
HALO = 128
ROWS = 112
MEMBERS = 8
CELLS = 1024
BLK = 256
STEPS = CELLS // BLK
HALF = 2 * BLK
HALVES = CELLS // HALF
PIECE = CELLS // MEMBERS
WIDE = D + 128

smoothing = 0.1
root_two_pi = math.sqrt(2.0 / math.pi)
cubic = 0.044715
epsilon = 1e-06
fair_shift = 0.05
fair_weight = 1.0 - fair_shift / MEMBERS
pair_coef = fair_weight / (2.0 * MEMBERS * (MEMBERS - 1))

bf16 = jnp.bfloat16
f32 = jnp.float32
VMEM_LIMIT = 24 * 1024 * 1024


def whole(shape):
    return pl.BlockSpec(shape, lambda *_: (0,) * len(shape), pipeline_mode=pl.Buffered(1))


def edge_matrix(neighbours, base, width):
    local = (neighbours - base).T
    shape = (local.shape[0], width)
    column = lax.broadcasted_iota(jnp.int32, shape, 1)
    row = lax.broadcasted_iota(jnp.int32, shape, 0)
    count = jnp.where(column == row + HALO, float(NBRS), 0.0)
    for k in range(NBRS):
        count = count + jnp.where(column == local[:, k : k + 1], 1.0, 0.0)
    return count.astype(bf16)


def gathered(edges, window):
    return jnp.dot(edges, window, preferred_element_type=f32) * (1.0 / NBRS)


def decode(combined, gain, mix, out_t, normed_ref, hidden_ref, deriv_ref, inv_ref, pred_ref, send_ref):
    inverse = lax.rsqrt(jnp.mean(combined * combined, axis=1, keepdims=True) + epsilon)
    normed = (combined * inverse * gain).astype(bf16)
    normed_ref[...] = normed
    inv_ref[...] = inverse
    x = jnp.dot(normed, mix(), preferred_element_type=f32)
    square = x * x
    tanh = jnp.tanh(x * (root_two_pi + (root_two_pi * cubic) * square))
    half = 0.5 + 0.5 * tanh
    activation = x * half
    deriv_ref[...] = (
        half + activation * (1.0 - tanh) * (root_two_pi + (3.0 * root_two_pi * cubic) * square)
    ).astype(bf16)
    hidden = (combined + activation).astype(bf16)
    hidden_ref[...] = hidden
    pred = lax.dot_general(out_t, hidden, (((1,), (1,)), ((), ())), preferred_element_type=f32)
    pred_ref[...] = pred
    rounded = pred.astype(bf16)
    for j in range(BLK // PIECE):
        send_ref[j] = rounded[:, j * PIECE : (j + 1) * PIECE]


def interior_kernel(
    nb0_ref, nb1_ref, gain_ref, out_ref, lat_hbm, mix_hbm,
    out_t_ref, lat, mix, normed_ref, hidden_ref, deriv_ref, inv_ref, pred_ref,
    *refs,
):
    send_ref, sems = refs
    step = pl.program_id(0)
    copies = [
        pltpu.make_async_copy(
            lat_hbm.at[i * BLK : (i + 1) * BLK], lat.at[i * BLK : (i + 1) * BLK], sems.at[i]
        )
        for i in range(STEPS)
    ] + [
        pltpu.make_async_copy(
            mix_hbm.at[i * BLK : (i + 1) * BLK], mix.at[i * BLK : (i + 1) * BLK], sems.at[STEPS + i]
        )
        for i in range(STEPS)
    ]
    first = pl.multiple_of(step * BLK, BLK)

    @pl.when(step == 0)
    def _():
        for at in (0, 1, 4, 5, 6, 7, 2, 3):
            copies[at].start()
        row = lax.broadcasted_iota(jnp.int32, (ROWS, VARS), 0)
        column = lax.broadcasted_iota(jnp.int32, (ROWS, VARS), 1)
        pick = jnp.where(row == column, 1.0, 0.0).astype(bf16)
        out_t_ref[...] = lax.dot_general(
            pick, out_ref[...], (((1,), (0,)), ((), ())), preferred_element_type=f32
        ).astype(bf16)

    neighbours = jnp.concatenate([nb0_ref[...], nb1_ref[...]], axis=1)
    base = lax.axis_index("space") * CELLS + first
    edges = edge_matrix(neighbours, base, BLK + 2 * HALO)

    @pl.when(step == 0)
    def _():
        for copy in copies[0:2]:
            copy.wait()

    @pl.when(step == 1)
    def _():
        copies[2].wait()

    @pl.when(step == 2)
    def _():
        copies[3].wait()

    def loaded_mix():
        @pl.when(step == 0)
        def _():
            for copy in copies[STEPS:]:
                copy.wait()

        return mix[...]

    combined = gathered(edges, lat[pl.ds(first, BLK + 2 * HALO)])
    decode(
        combined, gain_ref[...], loaded_mix, out_t_ref[...],
        normed_ref, hidden_ref, deriv_ref, inv_ref, pred_ref, send_ref,
    )


def rim_cells_kernel(
    nb0_ref, nb1_ref, lat_ref, near_ref, far_ref, gain_ref, mix_ref, out_t_ref,
    *refs,
):
    refs = refs[len(refs) // 2 :]
    space = lax.axis_index("space")
    start = space * CELLS
    first_core = lax.rem(space, 2) == 0
    low = jnp.where(first_core, far_ref[...], near_ref[...])
    high = jnp.where(first_core, near_ref[...], far_ref[...])
    last_edges = edge_matrix(nb0_ref[...], start + CELLS - BLK, BLK + HALO)
    head_edges = edge_matrix(nb1_ref[...], start - HALO, BLK + HALO)
    last = gathered(last_edges, jnp.concatenate([lat_ref[CELLS - BLK :], high], axis=0))
    head = gathered(head_edges, jnp.concatenate([low, lat_ref[0:BLK]], axis=0))
    combined = jnp.concatenate([last, head], axis=0)
    decode(combined, gain_ref[...], lambda: mix_ref[...], out_t_ref[...], *refs)


def in_hbm(value):
    return pltpu.with_memory_space_constraint(value, pltpu.HBM)


def forward(neighbours, center, near, far, gain, w_mix, w_out):
    shapes = [
        pltpu.HBM((CELLS, D), bf16),
        pltpu.HBM((CELLS, D), bf16),
        pltpu.HBM((CELLS, D), bf16),
        pltpu.HBM((CELLS, 1), f32),
        pltpu.HBM((ROWS, CELLS), f32),
        pltpu.HBM((MEMBERS, ROWS, PIECE), bf16),
    ]

    def blocks(at):
        rows = pl.BlockSpec((BLK, D), lambda i: (at(i), 0))
        return [
            rows,
            rows,
            rows,
            pl.BlockSpec((BLK, 1), lambda i: (at(i), 0)),
            pl.BlockSpec((ROWS, BLK), lambda i: (0, at(i))),
            pl.BlockSpec((BLK // PIECE, ROWS, PIECE), lambda i: (at(i), 0, 0)),
        ]

    def edges_at(column):
        return pl.BlockSpec((NBRS, PIECE), lambda i: (0, column(i)))

    def cost(steps):
        return pl.CostEstimate(
            flops=steps * 4 * BLK * D * D, bytes_accessed=steps * 3 << 20, transcendentals=steps * BLK * D
        )

    neighbours, gain = in_hbm(neighbours), in_hbm(gain)
    out_t, lat, mix, *arrays = pl.pallas_call(
        interior_kernel,
        grid=(STEPS - 1,),
        in_specs=[
            edges_at(lambda i: 2 * i + 1),
            edges_at(lambda i: 2 * i + 2),
            whole((1, D)),
            whole((VARS, D)),
            pl.BlockSpec(memory_space=pltpu.HBM),
            pl.BlockSpec(memory_space=pltpu.HBM),
        ],
        out_specs=[pl.BlockSpec(memory_space=pltpu.VMEM)] * 3 + blocks(lambda i: i),
        out_shape=[
            jax.ShapeDtypeStruct((ROWS, D), bf16),
            jax.ShapeDtypeStruct((CELLS, D), bf16),
            jax.ShapeDtypeStruct((D, D), bf16),
        ]
        + shapes,
        scratch_shapes=[
            pltpu.SemaphoreType.DMA((2 * STEPS,)),
        ],
        compiler_params=pltpu.CompilerParams(vmem_limit_bytes=VMEM_LIMIT),
        cost_estimate=cost(STEPS - 1),
        name="interior",
    )(neighbours, neighbours, gain, in_hbm(w_out), in_hbm(center), in_hbm(w_mix))
    arrays = pl.pallas_call(
        rim_cells_kernel,
        grid=(1,),
        in_specs=[
            edges_at(lambda i: MEMBERS - 1),
            edges_at(lambda i: 0),
            *[pl.BlockSpec(memory_space=pltpu.VMEM)] * 3,
            whole((1, D)),
            *[pl.BlockSpec(memory_space=pltpu.VMEM)] * 2,
        ]
        + [pl.BlockSpec(memory_space=pltpu.HBM)] * len(shapes),
        out_specs=blocks(lambda i: STEPS - 1),
        out_shape=shapes,
        input_output_aliases={8 + i: i for i in range(len(shapes))},
        compiler_params=pltpu.CompilerParams(vmem_limit_bytes=VMEM_LIMIT),
        cost_estimate=cost(1),
        name="rim_cells",
    )(neighbours, neighbours, lat, near, far, gain, mix, out_t, *arrays)
    return out_t, mix, arrays


def pair_kernel(pred_ref, obs_ref, area_ref, weight_ref, back_ref):
    area = area_ref[...]
    loss = jnp.zeros((16, PIECE), f32)
    for tile in range(ROWS // 16):
        rows = slice(16 * tile, 16 * tile + 16)
        preds = [pred_ref[m, rows].astype(f32) for m in range(MEMBERS)]
        observed = obs_ref[rows]
        slopes = [jnp.zeros((16, PIECE), f32)] * MEMBERS
        near = jnp.zeros((16, PIECE), f32)
        apart = jnp.zeros((16, PIECE), f32)
        for m in range(MEMBERS):
            gap = preds[m] - observed
            value = gap * gap + smoothing * smoothing
            near = near + value * lax.rsqrt(value)
            for k in range(m + 1, MEMBERS):
                gap = preds[m] - preds[k]
                value = gap * gap + smoothing * smoothing
                root = lax.rsqrt(value)
                apart = apart + value * root
                slope = gap * root
                slopes[m] = slopes[m] + slope
                slopes[k] = slopes[k] - slope
        loss = loss + weight_ref[rows] * (
            near * (1.0 / MEMBERS) - (2.0 * pair_coef) * apart
        )
        if tile < ROWS // 16 - 1:
            for m in range(MEMBERS):
                back_ref[m, rows] = slopes[m].astype(bf16)
    loss = jnp.sum(loss, axis=0, keepdims=True) * area
    high = loss.astype(bf16).astype(f32)
    middle = (loss - high).astype(bf16).astype(f32)
    low = loss - high - middle
    row = lax.broadcasted_iota(jnp.int32, (16, PIECE), 0) - (VARS - (ROWS - 16))
    for m in range(MEMBERS):
        tail = jnp.where(row < 0, slopes[m], 0.0)
        for at, part in enumerate((high, middle, low)):
            tail = jnp.where(row == at, part, tail)
        back_ref[m, ROWS - 16 : ROWS] = tail.astype(bf16)


def pair_terms(preds, observed, area, weight):
    column = lambda i: (0, lax.rem(lax.axis_index("member") + 1, MEMBERS))
    return pl.pallas_call(
        pair_kernel,
        grid=(1,),
        in_specs=[
            whole((MEMBERS, ROWS, PIECE)),
            pl.BlockSpec((ROWS, PIECE), column),
            pl.BlockSpec((1, PIECE), column),
            whole((ROWS, 1)),
        ],
        out_specs=whole((MEMBERS, ROWS, PIECE)),
        out_shape=pltpu.HBM((MEMBERS, ROWS, PIECE), bf16),
        cost_estimate=pl.CostEstimate(
            flops=1 << 24, bytes_accessed=1 << 20, transcendentals=1 << 20
        ),
        compiler_params=pltpu.CompilerParams(vmem_limit_bytes=VMEM_LIMIT),
        name="pairs",
    )(preds, in_hbm(observed), area, weight)


def weights_kernel(
    pos_ref, pair_ref, pred_ref, obs0_ref, obs1_ref, obs2_ref, obs3_ref,
    area0_ref, area1_ref, area2_ref, area3_ref, weight_ref, out_ref, deriv_ref,
    hidden0_ref, hidden1_ref, normed0_ref, normed1_ref,
    g_ref, pre_ref, loss_ref, keep_ref, send_ref, pre_all, g_all,
):
    step = pl.program_id(0)

    @pl.when(step < HALVES)
    def _():
        pair = jnp.concatenate([pair_ref[j] for j in range(HALF // PIECE)], axis=1).astype(f32)
        loss = jnp.sum(pair[VARS : VARS + 3], axis=0, keepdims=True)
        for j in range(HALF // PIECE):
            at = lax.rem(HALF // PIECE * step + 1 + j, MEMBERS) * PIECE
            loss_ref[:, pl.ds(pl.multiple_of(at, PIECE), PIECE)] = loss[:, j * PIECE : (j + 1) * PIECE]
        areas = (area0_ref, area1_ref, area2_ref, area3_ref)
        area = jnp.concatenate([ref[...] for ref in areas], axis=1)
        observed = (obs0_ref, obs1_ref, obs2_ref, obs3_ref)
        gap = pred_ref[...] - jnp.concatenate([ref[...] for ref in observed], axis=1)
        slope = gap * lax.rsqrt(gap * gap + smoothing * smoothing)
        g = (
            weight_ref[...]
            * area
            * (slope * (1.0 / MEMBERS) - (2.0 * pair_coef) * pair)
        ).astype(bf16)
        g_ref[...] = g
        d_hidden = lax.dot_general(
            g, out_ref[...], (((0,), (0,)), ((), ())), preferred_element_type=f32
        )
        d_pre = (d_hidden * deriv_ref[...].astype(f32)).astype(bf16)
        pre_ref[...] = d_pre
        rows = pl.ds(pl.multiple_of(step * HALF, HALF), HALF)
        pre_all[rows] = d_pre
        g_all[:, rows] = g

    @pl.when(step >= HALVES)
    def _():
        mine = pos_ref[2] == 0
        for x, hidden_ref, normed_ref in ((0, hidden0_ref, normed0_ref), (1, hidden1_ref, normed1_ref)):
            mix = lax.dot_general(
                normed_ref[...], pre_all[...], (((0,), (0,)), ((), ())), preferred_element_type=f32
            ).astype(bf16)
            out = jnp.dot(g_all[...], hidden_ref[...], preferred_element_type=f32)
            out = jnp.concatenate([out, jnp.zeros((128 - ROWS, BLK), f32)], axis=0).T.astype(bf16)
            for z in range(4):
                at = lax.rem(z + 4 - pos_ref[1], 4)
                for source, lanes in ((mix, slice(0, D)), (out, slice(D, WIDE))):
                    even = source[64 * z : 64 * z + 32]
                    odd = source[64 * z + 32 : 64 * z + 64]
                    keep_ref[x, at, :, lanes] = jnp.where(mine, even, odd)
                    send_ref[x, at, :, lanes] = jnp.where(mine, odd, even)


def weight_parts(pos, pair, pred, observed, area, weight, w_out, deriv, hidden, normed):
    first = lambda i: jnp.minimum(i, HALVES - 1)
    later = lambda i: jnp.maximum(i - HALVES, 0)
    rows = pl.BlockSpec((HALF, D), lambda i, pos: (first(i), 0))
    columns = pl.BlockSpec((ROWS, HALF), lambda i, pos: (0, first(i)))
    features = [
        pl.BlockSpec((CELLS, BLK), lambda i, pos, k=k: (0, lax.rem(pos[0] + 2 * later(i) + k, 4)))
        for k in (0, 1)
    ]
    pieces = HALF // PIECE
    places = [
        lambda i, pos, k=k: (0, lax.rem(pieces * first(i) + 1 + k, MEMBERS)) for k in range(pieces)
    ]
    share = pl.BlockSpec((2, 4, 32, WIDE), lambda i, pos: (later(i), 0, 0, 0))
    return pl.pallas_call(
        weights_kernel,
        grid_spec=pltpu.PrefetchScalarGridSpec(
            num_scalar_prefetch=1,
            grid=(HALVES + 2,),
            in_specs=[
                pl.BlockSpec((pieces, ROWS, PIECE), lambda i, pos: (first(i), 0, 0)),
                columns,
                *[pl.BlockSpec((ROWS, PIECE), place) for place in places],
                *[pl.BlockSpec((1, PIECE), place) for place in places],
                whole((ROWS, 1)),
                whole((ROWS, D)),
                rows,
                *features,
                *features,
            ],
            out_specs=[columns, rows, whole((1, CELLS)), share, share],
            scratch_shapes=[pltpu.VMEM((CELLS, D), bf16), pltpu.VMEM((ROWS, CELLS), bf16)],
        ),
        out_shape=[
            jax.ShapeDtypeStruct((ROWS, CELLS), bf16),
            jax.ShapeDtypeStruct((CELLS, D), bf16),
            jax.ShapeDtypeStruct((1, CELLS), f32),
            jax.ShapeDtypeStruct((4, 4, 32, WIDE), bf16),
            jax.ShapeDtypeStruct((4, 4, 32, WIDE), bf16),
        ],
        compiler_params=pltpu.CompilerParams(vmem_limit_bytes=VMEM_LIMIT),
        cost_estimate=pl.CostEstimate(
            flops=3 * CELLS * D * D, bytes_accessed=14 << 20, transcendentals=0
        ),
        name="weights",
    )(
        pos, pair, in_hbm(pred), *[in_hbm(observed)] * pieces, *[area] * pieces, weight, w_out,
        in_hbm(deriv), in_hbm(hidden), in_hbm(hidden), in_hbm(normed), in_hbm(normed),
    )


def latent_kernel(
    nb0_ref, nb1_ref, g_ref, out_ref, pre_ref, mix_ref, gain_ref, normed_ref, inv_ref,
    grad_ref, near_ref, far_ref, carry, tail,
):
    step = pl.program_id(0)
    d_hidden = lax.dot_general(
        g_ref[...], out_ref[...], (((0,), (0,)), ((), ())), preferred_element_type=f32
    )
    d_normed = lax.dot_general(
        pre_ref[...], mix_ref[...], (((1,), (1,)), ((), ())), preferred_element_type=f32
    )
    gain = gain_ref[...]
    normed = normed_ref[...].astype(f32)
    mean = jnp.mean(normed * d_normed, axis=1, keepdims=True)
    d_combined = d_hidden + inv_ref[...] * (d_normed * gain - normed * (1.0 / gain) * mean)
    d_combined = d_combined.astype(bf16)

    start = lax.axis_index("space") * CELLS

    def spread(edges, cells):
        return (1.0 / NBRS) * lax.dot_general(
            edges, cells, (((0,), (0,)), ((), ())), preferred_element_type=f32
        )

    @pl.when(step == 0)
    def _():
        edges = edge_matrix(nb0_ref[...], start + CELLS - BLK, BLK + HALO)
        last = spread(edges, d_combined[0:HALO])
        tail[...] = last[0:BLK]
        edges = edge_matrix(nb1_ref[...], start - HALO, BLK + HALO)
        head = spread(edges, d_combined[HALO:])
        carry[...] = head[HALO:]
        high, low = last[BLK:].astype(bf16), head[0:HALO].astype(bf16)
        first_core = lax.rem(lax.axis_index("space"), 2) == 0
        near_ref[...] = jnp.where(first_core, high, low)
        far_ref[...] = jnp.where(first_core, low, high)

    @pl.when(step > 0)
    def _():
        first = pl.multiple_of((step - 1) * BLK, BLK)
        neighbours = jnp.concatenate([nb0_ref[...], nb1_ref[...]], axis=1)
        part = spread(edge_matrix(neighbours, start + first, BLK + 2 * HALO), d_combined)
        grad_ref[pl.ds(first, BLK)] = (part[0:BLK] + carry[...]).astype(bf16)
        carry[...] = part[BLK:]

    @pl.when(step == STEPS - 1)
    def _():
        grad_ref[CELLS - BLK :] = (carry[...] + tail[...]).astype(bf16)


def latent_parts(neighbours, g, w_out, d_pre, w_mix, gain, normed, inverse):
    at = lambda i: lax.rem(i + STEPS - 1, STEPS)
    rows = pl.BlockSpec((BLK, D), lambda i: (at(i), 0))
    rim = jax.ShapeDtypeStruct((HALO, D), bf16)
    return pl.pallas_call(
        latent_kernel,
        grid=(STEPS,),
        in_specs=[
            pl.BlockSpec((NBRS, PIECE), lambda i: (0, 2 * at(i) + 1)),
            pl.BlockSpec((NBRS, PIECE), lambda i: (0, lax.rem(2 * at(i) + 2, MEMBERS))),
            pl.BlockSpec((ROWS, BLK), lambda i: (0, at(i))),
            whole((ROWS, D)),
            rows,
            whole((D, D)),
            whole((1, D)),
            rows,
            pl.BlockSpec((BLK, 1), lambda i: (at(i), 0)),
        ],
        out_specs=[whole((CELLS, D)), whole((HALO, D)), whole((HALO, D))],
        out_shape=[jax.ShapeDtypeStruct((CELLS, D), bf16), rim, rim],
        scratch_shapes=[pltpu.VMEM((BLK, D), f32), pltpu.VMEM((BLK, D), f32)],
        compiler_params=pltpu.CompilerParams(vmem_limit_bytes=VMEM_LIMIT),
        cost_estimate=pl.CostEstimate(
            flops=4 * CELLS * D * D, bytes_accessed=10 << 20, transcendentals=0
        ),
        name="latent",
    )(neighbours, neighbours, g, w_out, d_pre, w_mix, gain, normed, inverse)


def rim_kernel(grad_ref, near_ref, far_ref, out_ref):
    first_core = lax.rem(lax.axis_index("space"), 2) == 0
    other = jnp.where((pl.program_id(0) == 0) == first_core, far_ref[...], near_ref[...])
    out_ref[...] = (grad_ref[...].astype(f32) + other.astype(f32)).astype(bf16)


def add_rims(grad, near, far):
    rim = pl.BlockSpec((HALO, D), lambda i: (i * (CELLS // HALO - 1), 0))
    return pl.pallas_call(
        rim_kernel,
        grid=(2,),
        in_specs=[rim, whole((HALO, D)), whole((HALO, D))],
        out_specs=rim,
        out_shape=jax.ShapeDtypeStruct((CELLS, D), bf16),
        input_output_aliases={0: 0},
        compiler_params=pltpu.CompilerParams(vmem_limit_bytes=VMEM_LIMIT),
        cost_estimate=pl.CostEstimate(flops=1 << 18, bytes_accessed=3 << 19, transcendentals=0),
        name="rims",
    )(grad, near, far)


def along(value, axis, move):
    pairs = [(i, move(i)) for i in range(lax.axis_size(axis))]
    return lax.ppermute(value, axis, [pair for pair in pairs if pair[1] is not None])


def other_core(i):
    return i ^ 1


def other_chip(i):
    there = i + 1 if i % 2 else i - 1
    return there if 0 <= there < 32 else None


def summed(parts):
    total = parts[0].astype(f32)
    for part in parts[1:]:
        total = total + part.astype(f32)
    return total


def shards(latent, neighbours, norm_gain, w_mix, w_out, observed, cell_area, var_weight):
    space = lax.axis_index("space")
    pos = jnp.stack([space // 8, space // 2 % 4, space % 2]).astype(jnp.int32)
    center = latent[0]
    first_core = space % 2 == 0
    head, tail = center[:HALO], center[CELLS - HALO :]
    far = along(jnp.where(first_core, head, tail), "space", other_chip)
    near = along(jnp.where(first_core, tail, head), "space", other_core)
    gain = norm_gain.reshape(1, D)
    area = cell_area.reshape(1, CELLS)
    observed = jnp.pad(observed, ((0, ROWS - VARS), (0, 0)))
    weight = jnp.pad(var_weight, (0, ROWS - VARS)).reshape(ROWS, 1)

    out_t, mix, arrays = forward(neighbours, center, near, far, gain, w_mix, w_out.T)
    normed, hidden, deriv, inverse, pred, pieces = arrays
    pieces = lax.all_to_all(pieces, "member", 0, 0, tiled=True)
    pairs = pair_terms(pieces, observed, area, weight)
    pairs = lax.all_to_all(pairs, "member", 0, 0, tiled=True)
    g, d_pre, losses, keep, send = weight_parts(
        pos, pairs, pred, observed, area, weight, out_t, deriv, hidden, normed
    )
    got = along(send, "space", other_core)

    def own(k):
        return summed([keep[k], got[k]]).astype(bf16)

    def over_x(k, value):
        return along(value, "space", lambda i: (i + 8 * k) % 32)

    arrived = [over_x(k, own(k)) for k in (1, 2, 3)]
    grad, near, far = latent_parts(neighbours, g, out_t, d_pre, w_mix, gain, normed, inverse)
    arrived, grad = lax.optimization_barrier((arrived, grad))
    far = along(far, "space", other_chip)
    near = along(near, "space", other_core)
    share = summed([own(0)] + arrived).astype(bf16)

    def over_z(k):
        return along(share[k], "space", lambda i: i // 8 * 8 + (i + 2 * k) % 8)

    share = summed([share[0]] + [over_z(k) for k in (1, 2, 3)]).astype(bf16)
    arrived = [along(share, "member", lambda i: (i + 2 * k) % 8) for k in (1, 2, 3)]
    arrived, near, far = lax.optimization_barrier((arrived, near, far))
    share = summed([share] + arrived).astype(bf16)
    totals = summed([share, along(share, "member", lambda i: i ^ 1)])
    grad = add_rims(grad, near, far)
    grad_scale = 1.0 / math.sqrt(MEMBERS * CELLS * 32)
    return (
        losses.reshape(CELLS),
        grad[None],
        totals[:, :D] * grad_scale,
        totals[:, D : D + VARS] * grad_scale,
    )


def solution(mesh):
    return jax.shard_map(
        shards,
        mesh=mesh,
        in_specs=(
            P("member", "space", None),
            P(None, "space"),
            P(),
            P(),
            P(),
            P(None, "space"),
            P("space"),
            P(),
        ),
        out_specs=(P("space"), P("member", "space", None), P("space", None), P("space", None)),
        check_vma=False,
    )
```

```python
import math

import jax
import jax.numpy as jnp
from jax import lax
from jax.experimental import pallas as pl
from jax.experimental.pallas import tpu as pltpu
from jax.sharding import PartitionSpec as P

D = 1024
VARS = 100
NBRS = 4
HALO = 128
ROWS = 112
MEMBERS = 8
CELLS = 1024
BLK = 256
STEPS = CELLS // BLK
HALF = 2 * BLK
HALVES = CELLS // HALF
PIECE = CELLS // MEMBERS
WIDE = D + 128

smoothing = 0.1
root_two_pi = math.sqrt(2.0 / math.pi)
cubic = 0.044715
epsilon = 1e-06
fair_shift = 0.05
fair_weight = 1.0 - fair_shift / MEMBERS
pair_coef = fair_weight / (2.0 * MEMBERS * (MEMBERS - 1))
grad_scale = 1.0 / math.sqrt(MEMBERS * CELLS * 32)

bf16 = jnp.bfloat16
f32 = jnp.float32
VMEM_LIMIT = 24 * 1024 * 1024


def whole(shape):
    return pl.BlockSpec(shape, lambda *_: (0,) * len(shape), pipeline_mode=pl.Buffered(1))


def edge_matrix(neighbours, base, width):
    local = (neighbours - base).T
    shape = (local.shape[0], width)
    column = lax.broadcasted_iota(jnp.int32, shape, 1)
    row = lax.broadcasted_iota(jnp.int32, shape, 0)
    count = jnp.where(column == row + HALO, float(NBRS), 0.0)
    for k in range(NBRS):
        count = count + jnp.where(column == local[:, k : k + 1], 1.0, 0.0)
    return count.astype(bf16)


def gathered(edges, window):
    return jnp.dot(edges, window, preferred_element_type=f32) * (1.0 / NBRS)


def decode(combined, gain, mix, out_t, normed_ref, hidden_ref, deriv_ref, inv_ref, pred_ref, send_ref):
    inverse = lax.rsqrt(jnp.mean(combined * combined, axis=1, keepdims=True) + epsilon)
    normed = (combined * inverse * gain).astype(bf16)
    normed_ref[...] = normed
    inv_ref[...] = inverse
    x = jnp.dot(normed, mix(), preferred_element_type=f32)
    square = x * x
    tanh = jnp.tanh(x * (root_two_pi + (root_two_pi * cubic) * square))
    half = 0.5 + 0.5 * tanh
    activation = x * half
    deriv_ref[...] = (
        half + activation * (1.0 - tanh) * (root_two_pi + (3.0 * root_two_pi * cubic) * square)
    ).astype(bf16)
    hidden = (combined + activation).astype(bf16)
    hidden_ref[...] = hidden
    pred = lax.dot_general(out_t, hidden, (((1,), (1,)), ((), ())), preferred_element_type=f32)
    pred_ref[...] = pred
    rounded = pred.astype(bf16)
    for j in range(BLK // PIECE):
        send_ref[j] = rounded[:, j * PIECE : (j + 1) * PIECE]


def interior_kernel(
    nb0_ref, nb1_ref, gain_ref, out_ref, lat_hbm, mix_hbm,
    out_t_ref, lat, mix, normed_ref, hidden_ref, deriv_ref, inv_ref, pred_ref,
    *refs,
):
    send_ref, sems = refs
    step = pl.program_id(0)
    copies = [
        pltpu.make_async_copy(
            lat_hbm.at[i * BLK : (i + 1) * BLK], lat.at[i * BLK : (i + 1) * BLK], sems.at[i]
        )
        for i in range(STEPS)
    ] + [
        pltpu.make_async_copy(
            mix_hbm.at[i * BLK : (i + 1) * BLK], mix.at[i * BLK : (i + 1) * BLK], sems.at[STEPS + i]
        )
        for i in range(STEPS)
    ]
    first = pl.multiple_of(step * BLK, BLK)

    @pl.when(step == 0)
    def _():
        for at in (0, 1, 4, 5, 6, 7, 2, 3):
            copies[at].start()
        row = lax.broadcasted_iota(jnp.int32, (ROWS, VARS), 0)
        column = lax.broadcasted_iota(jnp.int32, (ROWS, VARS), 1)
        pick = jnp.where(row == column, 1.0, 0.0).astype(bf16)
        out_t_ref[...] = lax.dot_general(
            pick, out_ref[...], (((1,), (0,)), ((), ())), preferred_element_type=f32
        ).astype(bf16)

    neighbours = jnp.concatenate([nb0_ref[...], nb1_ref[...]], axis=1)
    base = lax.axis_index("space") * CELLS + first
    edges = edge_matrix(neighbours, base, BLK + 2 * HALO)

    @pl.when(step == 0)
    def _():
        for copy in copies[0:2]:
            copy.wait()

    @pl.when(step == 1)
    def _():
        copies[2].wait()

    @pl.when(step == 2)
    def _():
        copies[3].wait()

    def loaded_mix():
        @pl.when(step == 0)
        def _():
            for copy in copies[STEPS:]:
                copy.wait()

        return mix[...]

    combined = gathered(edges, lat[pl.ds(first, BLK + 2 * HALO)])
    decode(
        combined, gain_ref[...], loaded_mix, out_t_ref[...],
        normed_ref, hidden_ref, deriv_ref, inv_ref, pred_ref, send_ref,
    )


def rim_cells_kernel(
    nb0_ref, nb1_ref, lat_ref, near_ref, far_ref, gain_ref, mix_ref, out_t_ref,
    *refs,
):
    refs = refs[len(refs) // 2 :]
    space = lax.axis_index("space")
    start = space * CELLS
    first_core = lax.rem(space, 2) == 0
    low = jnp.where(first_core, far_ref[...], near_ref[...])
    high = jnp.where(first_core, near_ref[...], far_ref[...])
    last_edges = edge_matrix(nb0_ref[...], start + CELLS - BLK, BLK + HALO)
    head_edges = edge_matrix(nb1_ref[...], start - HALO, BLK + HALO)
    last = gathered(last_edges, jnp.concatenate([lat_ref[CELLS - BLK :], high], axis=0))
    head = gathered(head_edges, jnp.concatenate([low, lat_ref[0:BLK]], axis=0))
    combined = jnp.concatenate([last, head], axis=0)
    decode(combined, gain_ref[...], lambda: mix_ref[...], out_t_ref[...], *refs)


def in_hbm(value):
    return pltpu.with_memory_space_constraint(value, pltpu.HBM)


def forward(neighbours, center, near, far, gain, w_mix, w_out):
    shapes = [
        pltpu.HBM((CELLS, D), bf16),
        pltpu.HBM((CELLS, D), bf16),
        pltpu.HBM((CELLS, D), bf16),
        pltpu.HBM((CELLS, 1), f32),
        pltpu.HBM((ROWS, CELLS), f32),
        pltpu.HBM((MEMBERS, ROWS, PIECE), bf16),
    ]

    def blocks(at):
        rows = pl.BlockSpec((BLK, D), lambda i: (at(i), 0))
        return [
            rows,
            rows,
            rows,
            pl.BlockSpec((BLK, 1), lambda i: (at(i), 0)),
            pl.BlockSpec((ROWS, BLK), lambda i: (0, at(i))),
            pl.BlockSpec((BLK // PIECE, ROWS, PIECE), lambda i: (at(i), 0, 0)),
        ]

    def edges_at(column):
        return pl.BlockSpec((NBRS, PIECE), lambda i: (0, column(i)))

    def cost(steps):
        return pl.CostEstimate(
            flops=steps * 4 * BLK * D * D, bytes_accessed=steps * 3 << 20, transcendentals=steps * BLK * D
        )

    neighbours, gain = in_hbm(neighbours), in_hbm(gain)
    out_t, lat, mix, *arrays = pl.pallas_call(
        interior_kernel,
        grid=(STEPS - 1,),
        in_specs=[
            edges_at(lambda i: 2 * i + 1),
            edges_at(lambda i: 2 * i + 2),
            whole((1, D)),
            whole((VARS, D)),
            pl.BlockSpec(memory_space=pltpu.HBM),
            pl.BlockSpec(memory_space=pltpu.HBM),
        ],
        out_specs=[pl.BlockSpec(memory_space=pltpu.VMEM)] * 3 + blocks(lambda i: i),
        out_shape=[
            jax.ShapeDtypeStruct((ROWS, D), bf16),
            jax.ShapeDtypeStruct((CELLS, D), bf16),
            jax.ShapeDtypeStruct((D, D), bf16),
        ]
        + shapes,
        scratch_shapes=[
            pltpu.SemaphoreType.DMA((2 * STEPS,)),
        ],
        compiler_params=pltpu.CompilerParams(vmem_limit_bytes=VMEM_LIMIT),
        cost_estimate=cost(STEPS - 1),
        name="interior",
    )(neighbours, neighbours, gain, in_hbm(w_out), in_hbm(center), in_hbm(w_mix))
    arrays = pl.pallas_call(
        rim_cells_kernel,
        grid=(1,),
        in_specs=[
            edges_at(lambda i: MEMBERS - 1),
            edges_at(lambda i: 0),
            *[pl.BlockSpec(memory_space=pltpu.VMEM)] * 3,
            whole((1, D)),
            *[pl.BlockSpec(memory_space=pltpu.VMEM)] * 2,
        ]
        + [pl.BlockSpec(memory_space=pltpu.HBM)] * len(shapes),
        out_specs=blocks(lambda i: STEPS - 1),
        out_shape=shapes,
        input_output_aliases={8 + i: i for i in range(len(shapes))},
        compiler_params=pltpu.CompilerParams(vmem_limit_bytes=VMEM_LIMIT),
        cost_estimate=cost(1),
        name="rim_cells",
    )(neighbours, neighbours, lat, near, far, gain, mix, out_t, *arrays)
    return out_t, mix, arrays


def pair_kernel(pred_ref, obs_ref, area_ref, weight_ref, back_ref):
    area = area_ref[...]
    loss = jnp.zeros((16, PIECE), f32)
    for tile in range(ROWS // 16):
        rows = slice(16 * tile, 16 * tile + 16)
        preds = [pred_ref[m, rows].astype(f32) for m in range(MEMBERS)]
        observed = obs_ref[rows]
        slopes = [jnp.zeros((16, PIECE), f32)] * MEMBERS
        near = jnp.zeros((16, PIECE), f32)
        apart = jnp.zeros((16, PIECE), f32)
        for m in range(MEMBERS):
            gap = preds[m] - observed
            value = gap * gap + smoothing * smoothing
            near = near + value * lax.rsqrt(value)
            for k in range(m + 1, MEMBERS):
                gap = preds[m] - preds[k]
                value = gap * gap + smoothing * smoothing
                root = lax.rsqrt(value)
                apart = apart + value * root
                slope = gap * root
                slopes[m] = slopes[m] + slope
                slopes[k] = slopes[k] - slope
        loss = loss + weight_ref[rows] * (
            near * (1.0 / MEMBERS) - (2.0 * pair_coef) * apart
        )
        if tile < ROWS // 16 - 1:
            for m in range(MEMBERS):
                back_ref[m, rows] = slopes[m].astype(bf16)
    loss = jnp.sum(loss, axis=0, keepdims=True) * area
    high = loss.astype(bf16).astype(f32)
    middle = (loss - high).astype(bf16).astype(f32)
    low = loss - high - middle
    row = lax.broadcasted_iota(jnp.int32, (16, PIECE), 0) - (VARS - (ROWS - 16))
    for m in range(MEMBERS):
        tail = jnp.where(row < 0, slopes[m], 0.0)
        for at, part in enumerate((high, middle, low)):
            tail = jnp.where(row == at, part, tail)
        back_ref[m, ROWS - 16 : ROWS] = tail.astype(bf16)


def pair_terms(preds, observed, area, weight):
    column = lambda i: (0, lax.rem(lax.axis_index("member") + 1, MEMBERS))
    return pl.pallas_call(
        pair_kernel,
        grid=(1,),
        in_specs=[
            whole((MEMBERS, ROWS, PIECE)),
            pl.BlockSpec((ROWS, PIECE), column),
            pl.BlockSpec((1, PIECE), column),
            whole((ROWS, 1)),
        ],
        out_specs=whole((MEMBERS, ROWS, PIECE)),
        out_shape=pltpu.HBM((MEMBERS, ROWS, PIECE), bf16),
        cost_estimate=pl.CostEstimate(
            flops=1 << 24, bytes_accessed=1 << 20, transcendentals=1 << 20
        ),
        compiler_params=pltpu.CompilerParams(vmem_limit_bytes=VMEM_LIMIT),
        name="pairs",
    )(preds, in_hbm(observed), area, weight)


def weights_kernel(
    pos_ref, pair_ref, pred_ref, obs0_ref, obs1_ref, obs2_ref, obs3_ref,
    area0_ref, area1_ref, area2_ref, area3_ref, weight_ref, out_ref, deriv_ref,
    hidden0_ref, hidden1_ref, normed0_ref, normed1_ref,
    g_ref, pre_ref, loss_ref, keep_ref, send_ref, pre_all, g_all,
):
    step = pl.program_id(0)

    @pl.when(step < HALVES)
    def _():
        pair = jnp.concatenate([pair_ref[j] for j in range(HALF // PIECE)], axis=1).astype(f32)
        loss = jnp.sum(pair[VARS : VARS + 3], axis=0, keepdims=True)
        for j in range(HALF // PIECE):
            at = lax.rem(HALF // PIECE * step + 1 + j, MEMBERS) * PIECE
            loss_ref[:, pl.ds(pl.multiple_of(at, PIECE), PIECE)] = loss[:, j * PIECE : (j + 1) * PIECE]
        areas = (area0_ref, area1_ref, area2_ref, area3_ref)
        area = jnp.concatenate([ref[...] for ref in areas], axis=1)
        observed = (obs0_ref, obs1_ref, obs2_ref, obs3_ref)
        gap = pred_ref[...] - jnp.concatenate([ref[...] for ref in observed], axis=1)
        slope = gap * lax.rsqrt(gap * gap + smoothing * smoothing)
        g = (
            weight_ref[...]
            * area
            * (slope * (1.0 / MEMBERS) - (2.0 * pair_coef) * pair)
        ).astype(bf16)
        g_ref[...] = g
        d_hidden = lax.dot_general(
            g, out_ref[...], (((0,), (0,)), ((), ())), preferred_element_type=f32
        )
        d_pre = (d_hidden * deriv_ref[...].astype(f32)).astype(bf16)
        pre_ref[...] = d_pre
        rows = pl.ds(pl.multiple_of(step * HALF, HALF), HALF)
        pre_all[rows] = d_pre
        g_all[:, rows] = g

    @pl.when(step >= HALVES)
    def _():
        mine = pos_ref[2] == 0
        for x, hidden_ref, normed_ref in ((0, hidden0_ref, normed0_ref), (1, hidden1_ref, normed1_ref)):
            mix = lax.dot_general(
                normed_ref[...], pre_all[...], (((0,), (0,)), ((), ())), preferred_element_type=f32
            ).astype(bf16)
            out = jnp.dot(g_all[...], hidden_ref[...], preferred_element_type=f32)
            out = jnp.concatenate([out, jnp.zeros((128 - ROWS, BLK), f32)], axis=0).T.astype(bf16)
            for z in range(4):
                at = lax.rem(z + 4 - pos_ref[1], 4)
                for source, lanes in ((mix, slice(0, D)), (out, slice(D, WIDE))):
                    even = source[64 * z : 64 * z + 32]
                    odd = source[64 * z + 32 : 64 * z + 64]
                    keep_ref[x, at, :, lanes] = jnp.where(mine, even, odd)
                    send_ref[x, at, :, lanes] = jnp.where(mine, odd, even)


def weight_parts(pos, pair, pred, observed, area, weight, w_out, deriv, hidden, normed):
    first = lambda i: jnp.minimum(i, HALVES - 1)
    later = lambda i: jnp.maximum(i - HALVES, 0)
    rows = pl.BlockSpec((HALF, D), lambda i, pos: (first(i), 0))
    columns = pl.BlockSpec((ROWS, HALF), lambda i, pos: (0, first(i)))
    features = [
        pl.BlockSpec((CELLS, BLK), lambda i, pos, k=k: (0, lax.rem(pos[0] + 2 * later(i) + k, 4)))
        for k in (0, 1)
    ]
    pieces = HALF // PIECE
    places = [
        lambda i, pos, k=k: (0, lax.rem(pieces * first(i) + 1 + k, MEMBERS)) for k in range(pieces)
    ]
    share = pl.BlockSpec((2, 4, 32, WIDE), lambda i, pos: (later(i), 0, 0, 0))
    return pl.pallas_call(
        weights_kernel,
        grid_spec=pltpu.PrefetchScalarGridSpec(
            num_scalar_prefetch=1,
            grid=(HALVES + 2,),
            in_specs=[
                pl.BlockSpec((pieces, ROWS, PIECE), lambda i, pos: (first(i), 0, 0)),
                columns,
                *[pl.BlockSpec((ROWS, PIECE), place) for place in places],
                *[pl.BlockSpec((1, PIECE), place) for place in places],
                whole((ROWS, 1)),
                whole((ROWS, D)),
                rows,
                *features,
                *features,
            ],
            out_specs=[columns, rows, whole((1, CELLS)), share, share],
            scratch_shapes=[pltpu.VMEM((CELLS, D), bf16), pltpu.VMEM((ROWS, CELLS), bf16)],
        ),
        out_shape=[
            jax.ShapeDtypeStruct((ROWS, CELLS), bf16),
            jax.ShapeDtypeStruct((CELLS, D), bf16),
            jax.ShapeDtypeStruct((1, CELLS), f32),
            jax.ShapeDtypeStruct((4, 4, 32, WIDE), bf16),
            jax.ShapeDtypeStruct((4, 4, 32, WIDE), bf16),
        ],
        compiler_params=pltpu.CompilerParams(vmem_limit_bytes=VMEM_LIMIT),
        cost_estimate=pl.CostEstimate(
            flops=3 * CELLS * D * D, bytes_accessed=14 << 20, transcendentals=0
        ),
        name="weights",
    )(
        pos, pair, in_hbm(pred), *[in_hbm(observed)] * pieces, *[area] * pieces, weight, w_out,
        in_hbm(deriv), in_hbm(hidden), in_hbm(hidden), in_hbm(normed), in_hbm(normed),
    )


def latent_kernel(
    nb0_ref, nb1_ref, g_ref, out_ref, pre_ref, mix_ref, gain_ref, normed_ref, inv_ref,
    grad_ref, near_ref, far_ref, carry, tail,
):
    step = pl.program_id(0)
    d_hidden = lax.dot_general(
        g_ref[...], out_ref[...], (((0,), (0,)), ((), ())), preferred_element_type=f32
    )
    d_normed = lax.dot_general(
        pre_ref[...], mix_ref[...], (((1,), (1,)), ((), ())), preferred_element_type=f32
    )
    gain = gain_ref[...]
    normed = normed_ref[...].astype(f32)
    mean = jnp.mean(normed * d_normed, axis=1, keepdims=True)
    d_combined = d_hidden + inv_ref[...] * (d_normed * gain - normed * (1.0 / gain) * mean)
    d_combined = d_combined.astype(bf16)

    start = lax.axis_index("space") * CELLS

    def spread(edges, cells):
        return (1.0 / NBRS) * lax.dot_general(
            edges, cells, (((0,), (0,)), ((), ())), preferred_element_type=f32
        )

    @pl.when(step == 0)
    def _():
        edges = edge_matrix(nb0_ref[...], start + CELLS - BLK, BLK + HALO)
        last = spread(edges, d_combined[0:HALO])
        tail[...] = last[0:BLK]
        edges = edge_matrix(nb1_ref[...], start - HALO, BLK + HALO)
        head = spread(edges, d_combined[HALO:])
        carry[...] = head[HALO:]
        high, low = last[BLK:].astype(bf16), head[0:HALO].astype(bf16)
        first_core = lax.rem(lax.axis_index("space"), 2) == 0
        near_ref[...] = jnp.where(first_core, high, low)
        far_ref[...] = jnp.where(first_core, low, high)

    @pl.when(step > 0)
    def _():
        first = pl.multiple_of((step - 1) * BLK, BLK)
        neighbours = jnp.concatenate([nb0_ref[...], nb1_ref[...]], axis=1)
        part = spread(edge_matrix(neighbours, start + first, BLK + 2 * HALO), d_combined)
        grad_ref[pl.ds(first, BLK)] = (part[0:BLK] + carry[...]).astype(bf16)
        carry[...] = part[BLK:]

    @pl.when(step == STEPS - 1)
    def _():
        grad_ref[CELLS - BLK :] = (carry[...] + tail[...]).astype(bf16)


def latent_parts(neighbours, g, w_out, d_pre, w_mix, gain, normed, inverse):
    at = lambda i: lax.rem(i + STEPS - 1, STEPS)
    rows = pl.BlockSpec((BLK, D), lambda i: (at(i), 0))
    rim = jax.ShapeDtypeStruct((HALO, D), bf16)
    return pl.pallas_call(
        latent_kernel,
        grid=(STEPS,),
        in_specs=[
            pl.BlockSpec((NBRS, PIECE), lambda i: (0, 2 * at(i) + 1)),
            pl.BlockSpec((NBRS, PIECE), lambda i: (0, lax.rem(2 * at(i) + 2, MEMBERS))),
            pl.BlockSpec((ROWS, BLK), lambda i: (0, at(i))),
            whole((ROWS, D)),
            rows,
            whole((D, D)),
            whole((1, D)),
            rows,
            pl.BlockSpec((BLK, 1), lambda i: (at(i), 0)),
        ],
        out_specs=[whole((CELLS, D)), whole((HALO, D)), whole((HALO, D))],
        out_shape=[jax.ShapeDtypeStruct((CELLS, D), bf16), rim, rim],
        scratch_shapes=[pltpu.VMEM((BLK, D), f32), pltpu.VMEM((BLK, D), f32)],
        compiler_params=pltpu.CompilerParams(vmem_limit_bytes=VMEM_LIMIT),
        cost_estimate=pl.CostEstimate(
            flops=4 * CELLS * D * D, bytes_accessed=10 << 20, transcendentals=0
        ),
        name="latent",
    )(neighbours, neighbours, g, w_out, d_pre, w_mix, gain, normed, inverse)


def rim_kernel(grad_ref, near_ref, far_ref, out_ref):
    first_core = lax.rem(lax.axis_index("space"), 2) == 0
    other = jnp.where((pl.program_id(0) == 0) == first_core, far_ref[...], near_ref[...])
    out_ref[...] = (grad_ref[...].astype(f32) + other.astype(f32)).astype(bf16)


def add_rims(grad, near, far):
    rim = pl.BlockSpec((HALO, D), lambda i: (i * (CELLS // HALO - 1), 0))
    return pl.pallas_call(
        rim_kernel,
        grid=(2,),
        in_specs=[rim, whole((HALO, D)), whole((HALO, D))],
        out_specs=rim,
        out_shape=jax.ShapeDtypeStruct((CELLS, D), bf16),
        input_output_aliases={0: 0},
        compiler_params=pltpu.CompilerParams(vmem_limit_bytes=VMEM_LIMIT),
        cost_estimate=pl.CostEstimate(flops=1 << 18, bytes_accessed=3 << 19, transcendentals=0),
        name="rims",
    )(grad, near, far)


def finish_kernel(one_ref, two_ref, mix_ref, out_ref):
    total = (one_ref[...].astype(f32) + two_ref[...].astype(f32)) * grad_scale
    mix_ref[...] = total[:, :D]
    out_ref[...] = total[:, D : D + VARS]


def scaled_sum(one, two):
    return pl.pallas_call(
        finish_kernel,
        out_shape=[jax.ShapeDtypeStruct((32, D), f32), jax.ShapeDtypeStruct((32, VARS), f32)],
        compiler_params=pltpu.CompilerParams(vmem_limit_bytes=VMEM_LIMIT),
        cost_estimate=pl.CostEstimate(flops=1 << 17, bytes_accessed=1 << 18, transcendentals=0),
        name="finish",
    )(one, two)


def along(value, axis, move):
    pairs = [(i, move(i)) for i in range(lax.axis_size(axis))]
    return lax.ppermute(value, axis, [pair for pair in pairs if pair[1] is not None])


def other_core(i):
    return i ^ 1


def other_chip(i):
    there = i + 1 if i % 2 else i - 1
    return there if 0 <= there < 32 else None


def summed(parts):
    total = parts[0].astype(f32)
    for part in parts[1:]:
        total = total + part.astype(f32)
    return total


def shards(latent, neighbours, norm_gain, w_mix, w_out, observed, cell_area, var_weight):
    space = lax.axis_index("space")
    pos = jnp.stack([space // 8, space // 2 % 4, space % 2]).astype(jnp.int32)
    center = latent[0]
    first_core = space % 2 == 0
    head, tail = center[:HALO], center[CELLS - HALO :]
    far = along(jnp.where(first_core, head, tail), "space", other_chip)
    near = along(jnp.where(first_core, tail, head), "space", other_core)
    gain = norm_gain.reshape(1, D)
    area = cell_area.reshape(1, CELLS)
    observed = jnp.pad(observed, ((0, ROWS - VARS), (0, 0)))
    weight = jnp.pad(var_weight, (0, ROWS - VARS)).reshape(ROWS, 1)

    out_t, mix, arrays = forward(neighbours, center, near, far, gain, w_mix, w_out.T)
    normed, hidden, deriv, inverse, pred, pieces = arrays
    pieces = lax.all_to_all(pieces, "member", 0, 0, tiled=True)
    pairs = pair_terms(pieces, observed, area, weight)
    pairs = lax.all_to_all(pairs, "member", 0, 0, tiled=True)
    g, d_pre, losses, keep, send = weight_parts(
        pos, pairs, pred, observed, area, weight, out_t, deriv, hidden, normed
    )
    got = along(send, "space", other_core)

    def own(k):
        return summed([keep[k], got[k]]).astype(bf16)

    def over_x(k, value):
        return along(value, "space", lambda i: (i + 8 * k) % 32)

    arrived = [over_x(k, own(k)) for k in (1, 2, 3)]
    grad, near, far = latent_parts(neighbours, g, out_t, d_pre, w_mix, gain, normed, inverse)
    arrived, grad = lax.optimization_barrier((arrived, grad))
    far = along(far, "space", other_chip)
    near = along(near, "space", other_core)
    share = summed([own(0)] + arrived).astype(bf16)

    def over_z(k):
        return along(share[k], "space", lambda i: i // 8 * 8 + (i + 2 * k) % 8)

    share = summed([share[0]] + [over_z(k) for k in (1, 2, 3)]).astype(bf16)
    arrived = [along(share, "member", lambda i: (i + 2 * k) % 8) for k in (1, 2, 3)]
    arrived, near, far = lax.optimization_barrier((arrived, near, far))
    share = summed([share] + arrived).astype(bf16)
    mix_grad, out_grad = scaled_sum(share, along(share, "member", lambda i: i ^ 1))
    grad = add_rims(grad, near, far)
    return losses.reshape(CELLS), grad[None], mix_grad, out_grad


def solution(mesh):
    return jax.shard_map(
        shards,
        mesh=mesh,
        in_specs=(
            P("member", "space", None),
            P(None, "space"),
            P(),
            P(),
            P(),
            P(None, "space"),
            P("space"),
            P(),
        ),
        out_specs=(P("space"), P("member", "space", None), P("space", None), P("space", None)),
        check_vma=False,
    )
```
